256 devices in a mesh: pair: 64 (over z, y, core), red: 4 (over x).
Axes of the slice: x: 4, y: 4, z: 8, core: 2. Of those that a mesh axis runs over, the one named last changes fastest.
Arguments:
- ints: bfloat16 [4096, 64, 4096], P('pair', 'red'), may hold values from -6 to 6
- block_pairs: int32 [4096, 2], P('pair'), may hold values from 0 to 95
- block_dest: int32 [4096, 1], P('pair'), may hold values from 0 to 63; in each aligned block of 64 rows (0 to 63, 64 to 127, ...) at most 2 rows name the same one
- block_slot: int32 [4096], P('pair'), may hold values from 0 to 3
- occ_density: bfloat16 [96, 64, 64], replicated, may hold values from -0.75 to 0.75
- virt_density: bfloat16 [96, 64, 64], replicated, may hold values from -0.75 to 0.75
- isdf_cols: bfloat16 [96, 64, 256], replicated, may hold values from -0.375 to 0.375
- slab_cols: int32 [128], replicated, may hold values from 0 to 255
Outputs:
- chi_slab: bfloat16 [256, 64, 128], P('pair', 'red')
The draws below stay inside these ranges and needn't reach their ends.
Inputs may be any that keep to these rules, and one draw needn't show every extreme that they name: `block_dest`: among the 64 blocks of one index of pair (aligned blocks of rows) no owner is named more than 2 times, a bound that some block reaches.
All inputs are finite; a program needn't handle non-finite values.
Results may differ from the reference program's by a relative error of at most 0.015.
Values sent between devices are 32-bit elements; how exact they have to be, the bound alone decides.
A program may use at most 64 MiB of HBM per device.

```python
import math
import jax
import jax.numpy as jnp
import numpy as np
from jax import lax

BA = 64
NAB = 96
RS = 64
KB = 64
RB_DEV = 4
NQ = 128
NCAND = 256
NBLK = 4096
RB_TOTAL = 256
CAP = 2
N_PAIR = 64
N_RED = 4


def with_ends(entries, own_key, smallest, largest):
    longest = entries.shape.index(max(entries.shape))
    spots = []
    for shift in (0, 1):
        where = [jax.random.randint(jax.random.fold_in(own_key, axis), (), 0, length) for axis, length in enumerate(entries.shape)]
        where[longest] = (where[longest] + shift) % entries.shape[longest]
        spots.append(tuple(where))
    return entries.at[spots[0]].set(smallest).at[spots[1]].set(largest)


def block_levels(stream_key, dims, split, low, top_value):
    factor_of, own = 1.0, jax.random.fold_in(stream_key, 6)
    for dim, shards_of in split:
        steps = jnp.exp(jax.random.uniform(jax.random.fold_in(own, dim), (shards_of,), jnp.float32, low / len(split), top_value / len(split)))
        factor_of = factor_of * jnp.repeat(steps, dims[dim] // shards_of).reshape([-1 if axis == dim else 1 for axis in range(len(dims))])
    return factor_of


def shared_out(rng, own, number, rows, count, top, most, skew):
    sequence = jax.random.permutation(rng, count)
    crowded, usual = load_shares(count, rows * top, most, skew, True), load_shares(count, rows * top, most, skew, False)
    places = jnp.arange(count)

    def named(lengths, rotation):
        used = int((lengths > 0).sum())
        fixed = max(1, used // 4)
        shifted = fixed + (places - fixed + rotation * (used - fixed)) % max(1, count - fixed)
        return jnp.zeros((count,), jnp.int32).at[sequence[jnp.where(places < fixed, places, shifted)]].set(jnp.asarray(lengths, jnp.int32))

    lengths = jnp.where(number % 4 == 0, named(crowded, number // 4), named(usual, number - number // 4 - 1))
    mixed = jax.random.permutation(jax.random.fold_in(own, 3), count)
    donor, taker = mixed[0:count // 2 * 2:2], mixed[1:count // 2 * 2:2]
    margin = jnp.minimum(lengths[donor] - 1, most - lengths[taker]) // 2
    margin = jnp.where((donor == sequence[0]) | (taker == sequence[0]) | (lengths[taker] == 0), 0, jnp.maximum(margin, 0))
    shifted = jax.random.randint(jax.random.fold_in(own, 4), (count // 2,), 0, 1 << 20) % (margin + 1)
    lengths = lengths.at[donor].add(-shifted).at[taker].add(shifted)
    labels = jnp.searchsorted(jnp.cumsum(lengths), jnp.arange(rows * top), side="right").astype(jnp.int32)
    listing = labels.reshape(top, rows).T
    listing = listing[jax.random.permutation(jax.random.fold_in(own, 1), rows)]
    rotation = jax.random.randint(jax.random.fold_in(own, 2), (rows, 1), 0, top)
    return jnp.take_along_axis(listing, (jnp.arange(top)[None, :] + rotation) % top, axis=1)


def load_shares(count, total, reach, skew, full):
    portions = [(1 << 20) // math.isqrt(rank ** skew) + 1 for rank in range(1, count + 1)]
    largest = reach if full else min(reach, max(-(-total // count), total * portions[0] // sum(portions)))
    least = 1 if total - largest >= count - 1 else 0
    holding, spare = [largest] + [least] * (count - 1), total - largest - least * (count - 1)
    while spare > 0:
        free = [i for i in range(1, count) if holding[i] < largest] or [i for i in range(1, count) if holding[i] < reach]
        mass, remaining = sum([portions[i] for i in free]), spare
        for i in free:
            addition = min(reach - holding[i], max(1, remaining * portions[i] // mass), spare)
            holding[i] = holding[i] + addition
            spare = spare - addition
    return np.array(holding)


def gaussian(key, shape, width, bound, cuts=(), kind=jnp.bfloat16):
    gain = block_levels(key, shape, cuts, -0.22, 0.18) if cuts else 1.0
    values = jax.random.normal(key, shape, jnp.float32) * width * gain
    return jnp.minimum(jnp.maximum(values, -bound), bound).astype(kind)


def setup_inputs(seed: int = 0) -> dict:
    splits = jax.random.split(jax.random.key(seed), 9)
    ints = gaussian(splits[0], (NBLK, BA, RS * BA), 1.0, 6.0, ((0, 64), (1, 4)))
    block_pairs = with_ends(jax.random.randint(splits[1], (NBLK, 2), 0, NAB), jax.random.fold_in(splits[1], 1), 0, NAB - 1).astype(jnp.int32)
    block_dest_keys = jax.random.split(jax.random.fold_in(splits[2], 1), NBLK // KB)
    block_dest_turns = jax.random.permutation(jax.random.fold_in(splits[2], 3), NBLK // KB)
    block_dest = jax.vmap(lambda own, number: shared_out(jax.random.fold_in(splits[2], 2), own, number, KB, N_PAIR, 1, CAP, 2))(block_dest_keys, block_dest_turns).reshape((NBLK, 1))
    block_slot = with_ends(jax.random.randint(splits[3], (NBLK,), 0, RB_DEV), jax.random.fold_in(splits[3], 1), 0, RB_DEV - 1).astype(jnp.int32)
    occ_density = gaussian(splits[4], (NAB, BA, BA), BA ** -0.5, 0.75)
    virt_density = gaussian(splits[5], (NAB, BA, BA), BA ** -0.5, 0.75)
    isdf_cols = gaussian(splits[6], (NAB, BA, NCAND), (4 * BA) ** -0.5, 0.375)
    slab_cols = with_ends(jax.random.randint(splits[7], (NQ,), 0, NCAND), jax.random.fold_in(splits[7], 1), 0, NCAND - 1).astype(jnp.int32)
    return dict(ints=ints, block_pairs=block_pairs, block_dest=block_dest, block_slot=block_slot, occ_density=occ_density, virt_density=virt_density, isdf_cols=isdf_cols, slab_cols=slab_cols)


def reference(ints, block_pairs, block_dest, block_slot, occ_density, virt_density, isdf_cols, slab_cols):
    highest = lax.Precision.HIGHEST
    sel = jnp.take(isdf_cols, slab_cols, axis=2)
    occ_side = jnp.einsum('amn,amq->anq', occ_density.astype(jnp.float32), sel.astype(jnp.float32), precision=highest).astype(jnp.bfloat16)
    quarter = BA // N_RED

    def one_block(ints_b, pair):
        occ_b = occ_side[pair[0]].astype(jnp.float32)
        sel_b = sel[pair[1]].astype(jnp.float32)
        factor = (occ_b[:, None, :] * sel_b[None, :, :]).astype(jnp.bfloat16).reshape(BA * BA, NQ)
        virt_b = virt_density[pair[1]].astype(jnp.float32).reshape(N_RED, quarter, BA)
        pieces = ints_b.astype(jnp.float32).reshape(N_RED, quarter, RS * BA)
        half = jnp.einsum('glk,gls->gks', pieces, virt_b, precision=highest).astype(jnp.bfloat16)
        summed = jnp.sum(half.astype(jnp.float32), axis=0).reshape(RS, BA * BA)
        return jnp.dot(summed, factor.astype(jnp.float32), precision=highest)

    group_size = 8
    steps_count = NBLK // group_size
    ints_g = ints.reshape(steps_count, group_size, BA, RS * BA)
    pairs_g = block_pairs.reshape(steps_count, group_size, 2)
    rows_all = (block_dest[:, 0] * RB_DEV + block_slot).astype(jnp.int32)
    rows_g = rows_all.reshape(steps_count, group_size)

    def step_fn(carry, inputs):
        ints_s, pairs_s, rows_s = inputs
        parts = jax.vmap(one_block)(ints_s, pairs_s)
        return carry.at[rows_s].add(parts), None

    start = jnp.zeros((RB_TOTAL, RS, NQ), jnp.float32)
    chi, unused = lax.scan(step_fn, start, (ints_g, pairs_g, rows_g))
    return chi.astype(jnp.bfloat16)
```

```python
import functools

import jax
import jax.numpy as jnp
from jax import lax
from jax.experimental import pallas as pl
from jax.experimental.pallas import tpu as pltpu
from jax.sharding import PartitionSpec as P

MESH = pl.DeviceIdType.MESH
BF, F32 = jnp.bfloat16, jnp.float32

NB = 64
LAM = 16
BA = 64
NAB = 96
NQ = 128
NCAND = 256
PQ = 16
NX, NY, NZ = 4, 4, 8
SLOTS = 4
CB = 8
NCH = NB // CB
YC = 2
PC = PQ // YC


def kernel(
    ints_hbm, pairs_smem, pairs_ref, dest_ref, slot_ref, slab_ref, occ_hbm, virt_hbm, isdf_hbm,
    out_ref,
    ints, occ_t, virt_t, isdf, sel, dens, vdens, wbd, vside,
    parts, rxo, rxn, kown, koth, coreacc, dense, ryo, ryn, zbuf, zrecv, outf,
    load_sem, ints_sem, xs, xr, ks, kr, ys, yr, zs, zr,
):
    pair = lax.axis_index("pair")
    red = lax.axis_index("red")
    core = lax.rem(pair, 2)
    y = lax.rem(pair // 2, NY)
    z = pair // (2 * NY)

    def dev(zz, yy, cc, rr):
        return ((zz * NY + yy) * 2 + cc, rr)

    x_opp, x_r, x_l = lax.rem(red + 2, NX), lax.rem(red + 1, NX), lax.rem(red + 3, NX)
    y_opp, y_r, y_l = lax.rem(y + 2, NY), lax.rem(y + 1, NY), lax.rem(y + 3, NY)
    right_x, left_x = dev(z, y, core, x_r), dev(z, y, core, x_l)
    right_y, left_y = dev(z, y_r, core, red), dev(z, y_l, core, red)
    other = dev(z, y, 1 - core, red)

    loads = [
        pltpu.make_async_copy(isdf_hbm, isdf, load_sem.at[0]),
        pltpu.make_async_copy(virt_hbm.at[pl.ds(red * (LAM * BA), LAM * BA)], virt_t, load_sem.at[1]),
        pltpu.make_async_copy(occ_hbm, occ_t, load_sem.at[2]),
    ]
    for c in loads:
        c.start()

    def ints_copy(k):
        return pltpu.make_async_copy(
            ints_hbm.at[pl.ds(k * CB, CB)], ints.at[pl.ds(k * CB, CB)], ints_sem.at[k]
        )

    for k in range(NCH):
        ints_copy(k).start()

    barrier = pltpu.get_barrier_semaphore()
    peers = [right_x, left_x, right_y, left_y, other]
    peers += [dev(lax.rem(z + h, NZ), y, core, red) for h in range(1, NZ)]
    for d in peers:
        pl.semaphore_signal(barrier, inc=1, device_id=d, device_id_type=MESH)

    pick = (lax.broadcasted_iota(jnp.int32, (NCAND, NQ), 0) == slab_ref[...]).astype(F32).astype(BF)

    def one_hot_rows(row):
        wide = jnp.concatenate([pairs_ref[row : row + 1, :], jnp.full((1, 128 - NB), -1, jnp.int32)], axis=1)
        t = (lax.broadcasted_iota(jnp.int32, (128, 128), 0) == wide).astype(F32)
        return jnp.transpose(t)[:NB, :NAB].astype(BF)

    hot_i, hot_j = one_hot_rows(0), one_hot_rows(1)
    keys = dest_ref[...] * SLOTS + slot_ref[...]
    kown[...] = jnp.broadcast_to(jnp.concatenate([keys, keys], axis=1), (8, 128))

    loads[0].wait()
    rows = 512

    def sel_step(i, carry):
        at = pl.ds(pl.multiple_of(i * rows, rows), rows)
        got = jnp.dot(isdf[at, :], pick, preferred_element_type=F32).astype(BF)
        sel[pl.ds(i * (rows // BA), rows // BA)] = got.reshape(rows // BA, BA, NQ)
        return carry

    lax.fori_loop(0, NAB * BA // rows, sel_step, 0)

    low = lax.broadcasted_iota(jnp.int32, (NB, 128), 1) < BA

    def gathered(hot, src, dst, count):
        for tile in range(count * BA // 512):
            t = lax.dot_general(
                hot, src[tile * 512 : (tile + 1) * 512, :], (((1,), (1,)), ((), ())),
                preferred_element_type=F32,
            )
            for j in range(4):
                both = t[:, j * 128 : (j + 1) * 128]
                turned = pltpu.roll(both, BA, 1)
                m = tile * 8 + j * 2
                dst[pl.ds(m, NB, stride=count), :] = jnp.where(low, both, turned)
                dst[pl.ds(m + 1, NB, stride=count), :] = jnp.where(low, turned, both)

    loads[1].wait()
    gathered(hot_j, virt_t, vdens, LAM)
    loads[2].wait()
    gathered(hot_i, occ_t, dens, BA)

    top = lax.broadcasted_iota(jnp.int32, (2 * BA, NQ), 0) < BA

    def side_step(b, carry):
        first, second = pairs_smem[0, b], pairs_smem[1, b]
        sel_i, sel_j = sel[first], sel[second]
        d = dens[pl.ds(pl.multiple_of(b * BA, BA), BA), :].astype(BF)
        occ = lax.dot_general(d, sel_i, (((0,), (0,)), ((), ())), preferred_element_type=F32)
        wbd[b] = jnp.concatenate([jnp.where(top, occ, 0.0), jnp.where(top, 0.0, occ)], axis=1).astype(BF)
        v = vdens[pl.ds(pl.multiple_of(b * LAM, LAM), LAM), :BA].astype(BF)
        vside[b] = jnp.dot(v, sel_j, preferred_element_type=F32)
        return carry

    lax.fori_loop(0, NB, side_step, 0, unroll=4)

    def block_step(b, carry):
        x = ints[b]
        lhs = jnp.concatenate([x[:, i * 128 : (i + 1) * 128] for i in range(32)], axis=0)
        t = jnp.dot(lhs, wbd[b], preferred_element_type=F32)
        v = vside[b]
        vv = jnp.concatenate([v, v], axis=1)
        t = t.reshape(32, LAM, 2 * NQ) * vv[None]
        part = jnp.sum(t, axis=1)
        for r in range(NX):
            for lo in range(2):
                parts[pl.ds((r * PQ + lo * 8) * NB + b, 8, stride=NB), :] = part[r * 8 : r * 8 + 8, lo * NQ : (lo + 1) * NQ]
        return carry

    def remote(src, dst, send, recv, to):
        return pltpu.make_async_remote_copy(
            src_ref=src, dst_ref=dst, send_sem=send, recv_sem=recv, device_id=to, device_id_type=MESH
        )

    parts4 = parts.reshape(NX, PQ, NB, NQ)
    H = PQ // 2

    def x_copy(i, k):
        at = pl.ds(pl.multiple_of(k * CB, CB), CB)
        lo, hi = pl.ds(0, H), pl.ds(H, H)
        src, dst, to = {
            0: ((x_opp, lo, at), rxo.at[0, :, at], right_x),
            1: ((x_opp, hi, at), rxo.at[1, :, at], left_x),
            2: ((x_r, hi, at), rxn.at[0, hi, at], right_x),
            3: ((x_l, lo, at), rxn.at[1, lo, at], left_x),
            4: ((x_r, lo, at), rxn.at[0, lo, at], right_x),
            5: ((x_l, hi, at), rxn.at[1, hi, at], left_x),
            6: ((red, slice(None), at), coreacc.at[:, at], other),
        }[i]
        return remote(parts4.at[src], dst, xs.at[i, k], xr.at[i, k], to)

    pl.semaphore_wait(barrier, len(peers))
    key_copy = remote(kown, koth, ks.at[0], kr.at[0], other)
    key_copy.start()

    def chunk_step(t, carry):
        @pl.when(t < NCH)
        def _():
            ints_copy(t).wait()
            lax.fori_loop(t * CB, (t + 1) * CB, block_step, 0)
            for i in range(4):
                x_copy(i, t).start()

        @pl.when((t >= 1) & (t < NCH + 1))
        def _():
            k = t - 1
            at = pl.ds(pl.multiple_of(k * CB, CB), CB)
            x_copy(0, k).wait_recv()
            parts4[x_r, 0:H, at] += rxo[0, :, at]
            x_copy(4, k).start()
            x_copy(1, k).wait_recv()
            parts4[x_l, H:PQ, at] += rxo[1, :, at]
            x_copy(5, k).start()

        @pl.when(t >= 2)
        def _():
            k = t - 2
            at = pl.ds(pl.multiple_of(k * CB, CB), CB)
            for i in (2, 3, 4, 5):
                x_copy(i, k).wait_recv()
            parts4[red, :, at] += rxn[0, :, at] + rxn[1, :, at]
            x_copy(6, k).start()

        return carry

    lax.fori_loop(0, NCH + 2, chunk_step, 0)

    key_copy.wait()
    lane = lax.broadcasted_iota(jnp.int32, (1, 2 * NB), 1)
    both_keys = jnp.where(lane < NB, kown[0:1, :], koth[0:1, :])
    row = lax.broadcasted_iota(jnp.int32, (NY * NZ * SLOTS, 2 * NB), 0)
    ry, rz, rs = row // (NZ * SLOTS), (row // SLOTS) % NZ, row % SLOTS
    code = (((rz * NY) + ry) * 2 + core) * SLOTS + rs
    place = (code == both_keys).astype(F32).astype(BF)
    place2 = jnp.concatenate([place, place], axis=1)

    for k in range(NCH):
        x_copy(6, k).wait_recv()
    for p in range(0, PQ, 2):
        own = jnp.concatenate([parts4[red, p], parts4[red, p + 1]], axis=1)
        oth = jnp.concatenate([coreacc[p], coreacc[p + 1]], axis=1)
        both = jnp.concatenate([own, oth], axis=0)
        high = both.astype(BF)
        rest = (both - high.astype(F32)).astype(BF)
        d = jnp.dot(place2, jnp.concatenate([high, rest], axis=0), preferred_element_type=F32)
        dense[p] = d[:, :NQ].reshape(NY, NZ * SLOTS, NQ)
        dense[p + 1] = d[:, NQ:].reshape(NY, NZ * SLOTS, NQ)

    Q = PC // 2

    def y_copy(i, c):
        lo, hi = pl.ds(c * PC, Q), pl.ds(c * PC + Q, Q)
        src, dst, to = {
            0: ((lo, y_opp), ryo.at[0, c], right_y),
            1: ((hi, y_opp), ryo.at[1, c], left_y),
            2: ((hi, y_r), ryn.at[0, hi], right_y),
            3: ((lo, y_l), ryn.at[1, lo], left_y),
            4: ((lo, y_r), ryn.at[0, lo], right_y),
            5: ((hi, y_l), ryn.at[1, hi], left_y),
        }[i]
        return remote(dense.at[src], dst, ys.at[i, c], yr.at[i, c], to)

    def z_copy(h, c):
        zz = lax.rem(z + h, NZ)
        return remote(
            zbuf.at[c, zz], zrecv.at[c, z], zs.at[c, h], zr.at[c, z], dev(zz, y, core, red)
        )

    def z_wait(h, c):
        zz = lax.rem(z + h, NZ)
        remote(zbuf.at[c, zz], zrecv.at[c, zz], zs.at[c, h], zr.at[c, zz], other).wait_recv()

    zflat = zbuf.reshape(YC, NZ * SLOTS * PC, NQ)
    for c in range(YC):
        for i in range(4):
            y_copy(i, c).start()
    for c in range(YC):
        y_copy(0, c).wait_recv()
        dense[c * PC : c * PC + Q, y_r] += ryo[0, c]
        y_copy(4, c).start()
        y_copy(1, c).wait_recv()
        dense[c * PC + Q : (c + 1) * PC, y_l] += ryo[1, c]
        y_copy(5, c).start()
    for c in range(YC):
        for i in (2, 3, 4, 5):
            y_copy(i, c).wait_recv()
        for i in range(PC):
            p = c * PC + i
            zflat[c, pl.ds(i, NZ * SLOTS, stride=PC), :] = dense[p, y] + ryn[0, p] + ryn[1, p]
        for h in range(1, NZ):
            z_copy(h, c).start()
    for c in range(YC):
        for h in range(1, NZ):
            z_wait(h, c)
        total = zbuf[c, z]
        for h in range(1, NZ):
            total = total + zrecv[c, lax.rem(z + h, NZ)]
        outf[pl.ds(c, SLOTS * PC, stride=2), :] = total
    out_ref[...] = outf[...].astype(BF).reshape(SLOTS, PQ, NQ)

    def finish(k, carry):
        for i in range(7):
            x_copy(i, k).wait_send()
        return carry

    lax.fori_loop(0, NCH, finish, 0)
    for c in range(YC):
        for i in range(6):
            y_copy(i, c).wait_send()
        for h in range(1, NZ):
            z_copy(h, c).wait_send()


def shards(
    ints, block_pairs, block_dest, block_slot, occ_density, virt_density, isdf_cols, slab_cols
):
    hbm = pl.BlockSpec(memory_space=pl.ANY)
    vmem = pl.BlockSpec(memory_space=pltpu.VMEM)
    smem = pl.BlockSpec(memory_space=pltpu.SMEM)
    dma = pltpu.SemaphoreType.DMA
    pairs_t = block_pairs.T
    return pl.pallas_call(
        kernel,
        out_shape=jax.ShapeDtypeStruct((SLOTS, PQ, NQ), BF),
        in_specs=[hbm, smem, vmem, vmem, vmem, vmem, hbm, hbm, hbm],
        out_specs=vmem,
        scratch_shapes=[
            pltpu.VMEM((NB, LAM, BA * BA), BF),
            pltpu.VMEM((BA * BA, NAB), BF),
            pltpu.VMEM((LAM * BA, NAB), BF),
            pltpu.VMEM((NAB * BA, NCAND), BF),
            pltpu.VMEM((NAB, BA, NQ), BF),
            pltpu.VMEM((NB * BA, 2 * BA), F32),
            pltpu.VMEM((NB * LAM, 2 * BA), F32),
            pltpu.VMEM((NB, 2 * BA, 2 * NQ), BF),
            pltpu.VMEM((NB, LAM, NQ), F32),
            pltpu.VMEM((NX * PQ * NB, NQ), F32),
            pltpu.VMEM((2, PQ // 2, NB, NQ), F32),
            pltpu.VMEM((2, PQ, NB, NQ), F32),
            pltpu.VMEM((8, 128), jnp.int32),
            pltpu.VMEM((8, 128), jnp.int32),
            pltpu.VMEM((PQ, NB, NQ), F32),
            pltpu.VMEM((PQ, NY, NZ * SLOTS, NQ), F32),
            pltpu.VMEM((2, YC, PC // 2, NZ * SLOTS, NQ), F32),
            pltpu.VMEM((2, PQ, NZ * SLOTS, NQ), F32),
            pltpu.VMEM((YC, NZ, SLOTS * PC, NQ), F32),
            pltpu.VMEM((YC, NZ, SLOTS * PC, NQ), F32),
            pltpu.VMEM((SLOTS * PQ, NQ), F32),
            dma((3,)),
            dma((NCH,)),
            dma((7, NCH)),
            dma((7, NCH)),
            dma((1,)),
            dma((1,)),
            dma((6, YC)),
            dma((6, YC)),
            dma((YC, NZ)),
            dma((YC, NZ)),
        ],
        compiler_params=pltpu.CompilerParams(
            collective_id=0, has_side_effects=True, vmem_limit_bytes=56 * 1024 * 1024
        ),
        cost_estimate=pl.CostEstimate(flops=3_000_000_000, bytes_accessed=14_000_000, transcendentals=0),
    )(
        ints,
        pairs_t,
        pairs_t,
        block_dest.reshape(1, NB),
        block_slot.reshape(1, NB),
        slab_cols.reshape(1, NQ),
        occ_density.transpose(1, 2, 0).reshape(BA * BA, NAB),
        virt_density.transpose(1, 2, 0).reshape(BA * BA, NAB),
        isdf_cols.reshape(NAB * BA, NCAND),
    )


def solution(mesh):
    return jax.shard_map(
        shards,
        mesh=mesh,
        in_specs=(
            P("pair", "red", None),
            P("pair", None),
            P("pair", None),
            P("pair"),
            P(),
            P(),
            P(),
            P(),
        ),
        out_specs=P("pair", "red", None),
        check_vma=False,
    )
```

```python
import functools

import jax
import jax.numpy as jnp
from jax import lax
from jax.experimental import pallas as pl
from jax.experimental.pallas import tpu as pltpu
from jax.sharding import PartitionSpec as P

MESH = pl.DeviceIdType.MESH
BF, F32 = jnp.bfloat16, jnp.float32

NB = 64
LAM = 16
BA = 64
NAB = 96
NQ = 128
NCAND = 256
PQ = 16
NX, NY, NZ = 4, 4, 8
SLOTS = 4
CB = 8
NCH = NB // CB
GROUPS = ((0, 8), (8, 4), (12, 4))
NG = len(GROUPS)
CHUNKS = (8, 4, 1)
KEYS = NZ * SLOTS


def kernel(
    ints_hbm, pairs_smem, pairs_ref, dest_ref, slot_ref, slab_ref, occ_hbm, virt_hbm, isdf_hbm,
    out_ref,
    ints, occ_t, virt_t, isdf, dflat, vflat, dens, vdens, wbd, vside,
    parts, rxo, rxn, kown, koth, coreacc, dense, ryn, zbuf, zrecv, outf,
    load_sem, ints_sem, xs, xr, cs, cr, ks, kr, ys, yr, zs, zr,
):
    pair = lax.axis_index("pair")
    red = lax.axis_index("red")
    core = lax.rem(pair, 2)
    y = lax.rem(pair // 2, NY)
    z = pair // (2 * NY)

    def dev(zz, yy, cc, rr):
        return ((zz * NY + yy) * 2 + cc, rr)

    x_opp, x_r, x_l = lax.rem(red + 2, NX), lax.rem(red + 1, NX), lax.rem(red + 3, NX)
    right_x, left_x = dev(z, y, core, x_r), dev(z, y, core, x_l)
    other = dev(z, y, 1 - core, red)

    half = NAB // 2
    loads = [
        pltpu.make_async_copy(virt_hbm.at[pl.ds(red * (LAM * BA), LAM * BA)], virt_t, load_sem.at[0]),
        pltpu.make_async_copy(occ_hbm, occ_t, load_sem.at[1]),
        pltpu.make_async_copy(isdf_hbm.at[pl.ds(0, half)], isdf.at[pl.ds(0, half)], load_sem.at[2]),
        pltpu.make_async_copy(isdf_hbm.at[pl.ds(half, half)], isdf.at[pl.ds(half, half)], load_sem.at[3]),
    ]
    for c in loads:
        c.start()

    def ints_copy(k):
        return pltpu.make_async_copy(
            ints_hbm.at[pl.ds(k * CB, CB)], ints.at[pl.ds(k * CB, CB)], ints_sem.at[k]
        )

    ints_copy(0).start()

    barrier = pltpu.get_barrier_semaphore()
    peers = [right_x, left_x, other]
    peers += [dev(z, lax.rem(y + h, NY), core, red) for h in range(1, NY)]
    peers += [dev(lax.rem(z + h, NZ), y, core, red) for h in range(1, NZ)]
    for d in peers:
        pl.semaphore_signal(barrier, inc=1, device_id=d, device_id_type=MESH)

    pick = (lax.broadcasted_iota(jnp.int32, (NCAND, NQ), 0) == slab_ref[...]).astype(F32).astype(BF)

    def one_hot_rows(row):
        wide = jnp.concatenate([pairs_ref[row : row + 1, :], jnp.full((1, 128 - NB), -1, jnp.int32)], axis=1)
        t = (lax.broadcasted_iota(jnp.int32, (128, 128), 0) == wide).astype(F32)
        return jnp.transpose(t)[:NB, :NAB].astype(BF)

    hot_i, hot_j = one_hot_rows(0), one_hot_rows(1)
    keys = dest_ref[...] * SLOTS + slot_ref[...]
    kown[...] = jnp.broadcast_to(jnp.concatenate([keys, keys], axis=1), (8, 128))

    low = lax.broadcasted_iota(jnp.int32, (CB, 128), 1) < BA

    def gathered(hot, src, dst):
        for at in range(0, dst.shape[1], 512):
            dst[:, at : at + 512] = lax.dot_general(
                hot, src[at : at + 512, :], (((1,), (1,)), ((), ())), preferred_element_type=F32
            )

    def turned(flat, t, dst, count):
        at = pl.ds(pl.multiple_of(t * CB, CB), CB)
        for m in range(0, count, 2):
            both = flat[at, m * BA : (m + 2) * BA]
            back = pltpu.roll(both, BA, 1)
            dst[pl.ds(m, CB, stride=count), :] = jnp.where(low, both, back)
            dst[pl.ds(m + 1, CB, stride=count), :] = jnp.where(low, back, both)

    loads[0].wait()
    gathered(hot_j, virt_t, vflat)
    loads[1].wait()
    gathered(hot_i, occ_t, dflat)

    top = lax.broadcasted_iota(jnp.int32, (2 * BA, NQ), 0) < BA

    def sides(t):
        turned(vflat, t, vdens, LAM)
        turned(dflat, t, dens, BA)
        ids = [(pairs_smem[0, t * CB + i], pairs_smem[1, t * CB + i]) for i in range(CB)]
        cols = jnp.concatenate([isdf[a] for both in ids for a in both], axis=0)
        sel = jnp.dot(cols, pick, preferred_element_type=F32).astype(BF)
        for i in range(CB):
            b = t * CB + i
            sel_i, sel_j = sel[2 * i * BA : (2 * i + 1) * BA], sel[(2 * i + 1) * BA : (2 * i + 2) * BA]
            d = dens[i * BA : (i + 1) * BA, :].astype(BF)
            occ = lax.dot_general(d, sel_i, (((0,), (0,)), ((), ())), preferred_element_type=F32)
            wbd[b] = jnp.concatenate([jnp.where(top, occ, 0.0), jnp.where(top, 0.0, occ)], axis=1).astype(BF)
            v = vdens[i * LAM : (i + 1) * LAM, :BA].astype(BF)
            vside[b] = jnp.dot(v, sel_j, preferred_element_type=F32)

    sub = lax.broadcasted_iota(jnp.int32, (8, 2 * NQ), 0)

    def block_step(b, carry):
        x = ints[b]
        lhs = jnp.concatenate([x[:, i * 128 : (i + 1) * 128] for i in range(32)], axis=0)
        t = jnp.dot(lhs, wbd[b], preferred_element_type=F32)
        v = vside[b]
        v_lo = jnp.concatenate([v[:8], v[:8]], axis=1)
        v_hi = jnp.concatenate([v[8:], v[8:]], axis=1)
        tiles = [t[16 * p : 16 * p + 8] * v_lo + t[16 * p + 8 : 16 * p + 16] * v_hi for p in range(32)]
        for bit in range(3):
            mask = (sub & (1 << bit)) == 0
            tiles = [
                jnp.where(mask, a, c) + pltpu.roll(jnp.where(mask, c, a), 1 << bit, 0)
                for a, c in zip(tiles[0::2], tiles[1::2])
            ]
        for r in range(NX):
            for lo in range(2):
                parts[pl.ds((r * PQ + lo * 8) * NB + b, 8, stride=NB), :] = tiles[r][:, lo * NQ : (lo + 1) * NQ]
        return carry

    def remote(src, dst, send, recv, to):
        return pltpu.make_async_remote_copy(
            src_ref=src, dst_ref=dst, send_sem=send, recv_sem=recv, device_id=to, device_id_type=MESH
        )

    parts4 = parts.reshape(NX, PQ, NB, NQ)

    def span(g, k):
        n = NB // CHUNKS[g]
        return pl.ds(pl.multiple_of(k * n, n), n)

    def halves(g):
        p0, n = GROUPS[g]
        return pl.ds(p0, n // 2), pl.ds(p0 + n // 2, n // 2)

    def x_copy(g, i, k):
        at = span(g, k)
        lo, hi = halves(g)
        src, dst, to = {
            0: ((x_opp, lo, at), rxo.at[lo, at], right_x),
            1: ((x_opp, hi, at), rxo.at[hi, at], left_x),
            2: ((x_r, hi, at), rxn.at[0, hi, at], right_x),
            3: ((x_l, lo, at), rxn.at[1, lo, at], left_x),
            4: ((x_r, lo, at), rxn.at[0, lo, at], right_x),
            5: ((x_l, hi, at), rxn.at[1, hi, at], left_x),
        }[i]
        return remote(parts4.at[src], dst, xs.at[g, i, k], xr.at[g, i, k], to)

    def x_first(g, k):
        for i in range(4):
            x_copy(g, i, k).start()

    def x_second(g, k):
        at = span(g, k)
        lo, hi = halves(g)
        x_copy(g, 0, k).wait_recv()
        parts4[x_r, lo, at] += rxo[lo, at]
        x_copy(g, 4, k).start()
        x_copy(g, 1, k).wait_recv()
        parts4[x_l, hi, at] += rxo[hi, at]
        x_copy(g, 5, k).start()

    def core_copy(g):
        ps = pl.ds(*GROUPS[g])
        return remote(parts4.at[red, ps], coreacc.at[ps], cs.at[g], cr.at[g], other)

    def x_last(g):
        def one(k, carry):
            for i in (2, 3, 4, 5):
                x_copy(g, i, k).wait_recv()
            return carry

        lax.fori_loop(0, CHUNKS[g], one, 0)
        ps = pl.ds(*GROUPS[g])
        parts4[red, ps] += rxn[0, ps] + rxn[1, ps]
        core_copy(g).start()

    def compute(t):
        ints_copy(t).wait()
        sides(t)
        lax.fori_loop(0, CB, lambda i, carry: block_step(t * CB + i, carry), 0, unroll=CB)

    loads[2].wait()
    loads[3].wait()
    for k in range(1, NCH):
        ints_copy(k).start()
    compute(0)
    pl.semaphore_wait(barrier, len(peers))
    key_copy = remote(kown, koth, ks.at[0], kr.at[0], other)
    key_copy.start()
    x_first(0, 0)

    def chunk_step(t, carry):
        compute(t)
        x_first(0, t)

        @pl.when(t >= 2)
        def _():
            x_second(0, t - 2)

        @pl.when(t % 2 == 1)
        def _():
            x_first(1, t // 2)

        return carry

    lax.fori_loop(1, NCH, chunk_step, 0)

    def many(g, first, last):
        def one(k, carry):
            x_second(g, k)
            return carry

        lax.fori_loop(first, last, one, 0)

    key_copy.wait()
    lane = lax.broadcasted_iota(jnp.int32, (1, 2 * NB), 1)
    both_keys = jnp.where(lane < NB, kown[0:1, :], koth[0:1, :])
    row = lax.broadcasted_iota(jnp.int32, (NY * KEYS, 2 * NB), 0)
    ry, rz, rs = row // KEYS, (row // SLOTS) % NZ, row % SLOTS
    code = (((rz * NY) + ry) * 2 + core) * SLOTS + rs
    place = (code == both_keys).astype(F32).astype(BF)
    place2 = jnp.concatenate([place, place], axis=1)

    def y_copy(g, h):
        ps = pl.ds(*GROUPS[g])
        yy = lax.rem(y + h, NY)
        return remote(dense.at[ps, yy], ryn.at[y, ps], ys.at[g, h], yr.at[g, y], dev(z, yy, core, red))

    def y_wait(g, h):
        ps = pl.ds(*GROUPS[g])
        yy = lax.rem(y + h, NY)
        remote(dense.at[ps, yy], ryn.at[yy, ps], ys.at[g, h], yr.at[g, yy], other).wait_recv()

    def densify(g):
        p0, n = GROUPS[g]
        core_copy(g).wait_recv()
        for p in range(p0, p0 + n, 2):
            own = jnp.concatenate([parts4[red, p], parts4[red, p + 1]], axis=1)
            oth = jnp.concatenate([coreacc[p], coreacc[p + 1]], axis=1)
            both = jnp.concatenate([own, oth], axis=0)
            high = both.astype(BF)
            rest = (both - high.astype(F32)).astype(BF)
            d = jnp.dot(place2, jnp.concatenate([high, rest], axis=0), preferred_element_type=F32)
            dense[p] = d[:, :NQ].reshape(NY, KEYS, NQ)
            dense[p + 1] = d[:, NQ:].reshape(NY, KEYS, NQ)
        for h in range(1, NY):
            y_copy(g, h).start()

    def z_rows(g):
        p0, n = GROUPS[g]
        return pl.ds(p0 * SLOTS, n * SLOTS)

    def z_copy(g, h):
        zz = lax.rem(z + h, NZ)
        at = z_rows(g)
        return remote(zbuf.at[zz, at], zrecv.at[z, at], zs.at[g, h], zr.at[g, z], dev(zz, y, core, red))

    def z_wait(g, h):
        zz = lax.rem(z + h, NZ)
        at = z_rows(g)
        remote(zbuf.at[zz, at], zrecv.at[zz, at], zs.at[g, h], zr.at[g, zz], other).wait_recv()

    zflat = zbuf.reshape(NZ * SLOTS * PQ, NQ)

    def y_last(g):
        p0, n = GROUPS[g]
        for h in range(1, NY):
            y_wait(g, h)
        for i in range(n):
            p = p0 + i
            total = dense[p, y]
            for h in range(1, NY):
                total = total + ryn[lax.rem(y + h, NY), p]
            for zz in range(NZ):
                zflat[pl.ds(zz * SLOTS * PQ + p0 * SLOTS + i, SLOTS, stride=n), :] = total[zz * SLOTS : (zz + 1) * SLOTS]
        for h in range(1, NZ):
            z_copy(g, h).start()

    def z_last(g):
        p0, n = GROUPS[g]
        for h in range(1, NZ):
            z_wait(g, h)
        at = z_rows(g)
        total = zbuf[z, at]
        for h in range(1, NZ):
            total = total + zrecv[lax.rem(z + h, NZ), at]
        lo, i0 = p0 // 8, p0 % 8
        for slot in range(SLOTS):
            outf[pl.ds(slot * PQ + 2 * i0 + lo, n, stride=2), :] = total[slot * n : (slot + 1) * n]

    def x_sent(g):
        def one(k, carry):
            for i in range(6):
                x_copy(g, i, k).wait_send()
            return carry

        lax.fori_loop(0, CHUNKS[g], one, 0)
        core_copy(g).wait_send()

    many(0, NCH - 2, NCH)
    x_first(2, 0)
    many(1, 0, CHUNKS[1])
    x_last(0)
    densify(0)
    x_second(2, 0)
    x_last(1)
    densify(1)
    y_last(0)
    x_sent(0)
    x_last(2)
    densify(2)
    x_sent(1)
    x_sent(2)
    y_last(1)
    z_last(0)
    y_last(2)
    z_last(1)
    z_last(2)
    out_ref[...] = outf[...].astype(BF).reshape(SLOTS, PQ, NQ)

    for g in range(NG):
        for h in range(1, NY):
            y_copy(g, h).wait_send()
        for h in range(1, NZ):
            z_copy(g, h).wait_send()


def shards(
    ints, block_pairs, block_dest, block_slot, occ_density, virt_density, isdf_cols, slab_cols
):
    hbm = pl.BlockSpec(memory_space=pl.ANY)
    vmem = pl.BlockSpec(memory_space=pltpu.VMEM)
    smem = pl.BlockSpec(memory_space=pltpu.SMEM)
    dma = pltpu.SemaphoreType.DMA
    pairs_t = block_pairs.T
    return pl.pallas_call(
        kernel,
        out_shape=jax.ShapeDtypeStruct((SLOTS, PQ, NQ), BF),
        in_specs=[hbm, smem, vmem, vmem, vmem, vmem, hbm, hbm, hbm],
        out_specs=vmem,
        scratch_shapes=[
            pltpu.VMEM((NB, LAM, BA * BA), BF),
            pltpu.VMEM((BA * BA, NAB), BF),
            pltpu.VMEM((LAM * BA, NAB), BF),
            pltpu.VMEM((NAB, BA, NCAND), BF),
            pltpu.VMEM((NB, BA * BA), F32),
            pltpu.VMEM((NB, LAM * BA), F32),
            pltpu.VMEM((CB * BA, 2 * BA), F32),
            pltpu.VMEM((CB * LAM, 2 * BA), F32),
            pltpu.VMEM((NB, 2 * BA, 2 * NQ), BF),
            pltpu.VMEM((NB, LAM, NQ), F32),
            pltpu.VMEM((NX * PQ * NB, NQ), F32),
            pltpu.VMEM((PQ, NB, NQ), F32),
            pltpu.VMEM((2, PQ, NB, NQ), F32),
            pltpu.VMEM((8, 128), jnp.int32),
            pltpu.VMEM((8, 128), jnp.int32),
            pltpu.VMEM((PQ, NB, NQ), F32),
            pltpu.VMEM((PQ, NY, KEYS, NQ), F32),
            pltpu.VMEM((NY, PQ, KEYS, NQ), F32),
            pltpu.VMEM((NZ, SLOTS * PQ, NQ), F32),
            pltpu.VMEM((NZ, SLOTS * PQ, NQ), F32),
            pltpu.VMEM((SLOTS * PQ, NQ), F32),
            dma((4,)),
            dma((NCH,)),
            dma((NG, 6, NCH)),
            dma((NG, 6, NCH)),
            dma((NG,)),
            dma((NG,)),
            dma((1,)),
            dma((1,)),
            dma((NG, NY)),
            dma((NG, NY)),
            dma((NG, NZ)),
            dma((NG, NZ)),
        ],
        compiler_params=pltpu.CompilerParams(
            collective_id=0, has_side_effects=True, vmem_limit_bytes=56 * 1024 * 1024
        ),
        cost_estimate=pl.CostEstimate(flops=3_000_000_000, bytes_accessed=14_000_000, transcendentals=0),
    )(
        ints,
        pairs_t,
        pairs_t,
        block_dest.reshape(1, NB),
        block_slot.reshape(1, NB),
        slab_cols.reshape(1, NQ),
        occ_density.transpose(1, 2, 0).reshape(BA * BA, NAB),
        virt_density.transpose(1, 2, 0).reshape(BA * BA, NAB),
        isdf_cols,
    )


def solution(mesh):
    return jax.shard_map(
        shards,
        mesh=mesh,
        in_specs=(
            P("pair", "red", None),
            P("pair", None),
            P("pair", None),
            P("pair"),
            P(),
            P(),
            P(),
            P(),
        ),
        out_specs=P("pair", "red", None),
        check_vma=False,
    )
```

```python
import functools

import jax
import jax.numpy as jnp
from jax import lax
from jax.experimental import pallas as pl
from jax.experimental.pallas import tpu as pltpu
from jax.sharding import PartitionSpec as P

MESH = pl.DeviceIdType.MESH
BF, F32 = jnp.bfloat16, jnp.float32

NB = 64
LAM = 16
BA = 64
NAB = 96
NQ = 128
NCAND = 256
PQ = 16
NX, NY, NZ = 4, 4, 8
SLOTS = 4
CB = 8
NCH = NB // CB
GROUPS = ((0, 8), (8, 4), (12, 4))
NG = len(GROUPS)
RELAYED = (True, False, False)
CHUNKS = (8, 4, 1)
KEYS = NZ * SLOTS


def kernel(
    ints_hbm, pairs_hbm, dest_hbm, slot_hbm, slab_hbm, occ_hbm, virt_hbm, isdf_hbm,
    out_ref,
    pairs_smem, pairs_ref, dest_ref, slot_ref, slab_ref, ints, occ_t, virt_t, isdf, dflat, vflat, dens, vdens, wbd, vside,
    parts, rxo, rxn, kown, koth, coreacc, dense, ryo, ryn, ryd, zbuf, zrecv, outf,
    small_sem, load_sem, ints_sem, xs, xr, cs, cr, ks, kr, ys, yr, zs, zr,
):
    pair = lax.axis_index("pair")
    red = lax.axis_index("red")
    core = lax.rem(pair, 2)
    y = lax.rem(pair // 2, NY)
    z = pair // (2 * NY)

    def dev(zz, yy, cc, rr):
        return ((zz * NY + yy) * 2 + cc, rr)

    y_opp, y_r, y_l = lax.rem(y + 2, NY), lax.rem(y + 1, NY), lax.rem(y + 3, NY)
    x_opp, x_r, x_l = lax.rem(red + 2, NX), lax.rem(red + 1, NX), lax.rem(red + 3, NX)
    right_x, left_x = dev(z, y, core, x_r), dev(z, y, core, x_l)
    right_y, left_y = dev(z, y_r, core, red), dev(z, y_l, core, red)
    other = dev(z, y, 1 - core, red)

    small = [
        pltpu.make_async_copy(src, dst, small_sem.at[i])
        for i, (src, dst) in enumerate(
            (
                (pairs_hbm, pairs_ref),
                (slab_hbm, slab_ref),
                (dest_hbm, dest_ref),
                (slot_hbm, slot_ref),
                (pairs_hbm, pairs_smem),
            )
        )
    ]
    for c in small:
        c.start()
    half = NAB // 2
    loads = [
        pltpu.make_async_copy(virt_hbm.at[pl.ds(red * (LAM * BA), LAM * BA)], virt_t, load_sem.at[0]),
        pltpu.make_async_copy(occ_hbm, occ_t, load_sem.at[1]),
        pltpu.make_async_copy(isdf_hbm.at[pl.ds(0, half)], isdf.at[pl.ds(0, half)], load_sem.at[2]),
        pltpu.make_async_copy(isdf_hbm.at[pl.ds(half, half)], isdf.at[pl.ds(half, half)], load_sem.at[3]),
    ]
    for c in loads:
        c.start()

    def ints_copy(k):
        return pltpu.make_async_copy(
            ints_hbm.at[pl.ds(k * CB, CB)], ints.at[pl.ds(k * CB, CB)], ints_sem.at[k]
        )

    ints_copy(0).start()

    barrier = pltpu.get_barrier_semaphore()
    peers = [right_x, left_x, right_y, left_y, dev(z, y_opp, core, red), other]
    peers += [dev(lax.rem(z + h, NZ), y, core, red) for h in range(1, NZ)]
    for d in peers:
        pl.semaphore_signal(barrier, inc=1, device_id=d, device_id_type=MESH)

    for c in small:
        c.wait()
    pick = (lax.broadcasted_iota(jnp.int32, (NCAND, NQ), 0) == slab_ref[...]).astype(F32).astype(BF)

    def one_hot_rows(row):
        wide = jnp.concatenate([pairs_ref[row : row + 1, :], jnp.full((1, 128 - NB), -1, jnp.int32)], axis=1)
        t = (lax.broadcasted_iota(jnp.int32, (128, 128), 0) == wide).astype(F32)
        return jnp.transpose(t)[:NB, :NAB].astype(BF)

    hot_i, hot_j = one_hot_rows(0), one_hot_rows(1)
    keys = dest_ref[...] * SLOTS + slot_ref[...]
    kown[...] = jnp.broadcast_to(jnp.concatenate([keys, keys], axis=1), (8, 128))

    low = lax.broadcasted_iota(jnp.int32, (CB, 128), 1) < BA

    def gathered(hot, src, dst):
        for at in range(0, dst.shape[1], 512):
            dst[:, at : at + 512] = lax.dot_general(
                hot, src[at : at + 512, :], (((1,), (1,)), ((), ())), preferred_element_type=F32
            )

    def turned(flat, t, dst, count):
        at = pl.ds(pl.multiple_of(t * CB, CB), CB)
        for m in range(0, count, 2):
            both = flat[at, m * BA : (m + 2) * BA]
            back = pltpu.roll(both, BA, 1)
            dst[pl.ds(m, CB, stride=count), :] = jnp.where(low, both, back)
            dst[pl.ds(m + 1, CB, stride=count), :] = jnp.where(low, back, both)

    loads[0].wait()
    gathered(hot_j, virt_t, vflat)
    loads[1].wait()
    gathered(hot_i, occ_t, dflat)

    top = lax.broadcasted_iota(jnp.int32, (2 * BA, NQ), 0) < BA

    def sides(t):
        turned(vflat, t, vdens, LAM)
        turned(dflat, t, dens, BA)
        ids = [(pairs_smem[0, t * CB + i], pairs_smem[1, t * CB + i]) for i in range(CB)]
        cols = jnp.concatenate([isdf[a] for both in ids for a in both], axis=0)
        sel = jnp.dot(cols, pick, preferred_element_type=F32).astype(BF)
        for i in range(CB):
            b = t * CB + i
            sel_i, sel_j = sel[2 * i * BA : (2 * i + 1) * BA], sel[(2 * i + 1) * BA : (2 * i + 2) * BA]
            d = dens[i * BA : (i + 1) * BA, :].astype(BF)
            occ = lax.dot_general(d, sel_i, (((0,), (0,)), ((), ())), preferred_element_type=F32)
            wbd[b] = jnp.concatenate([jnp.where(top, occ, 0.0), jnp.where(top, 0.0, occ)], axis=1).astype(BF)
            v = vdens[i * LAM : (i + 1) * LAM, :BA].astype(BF)
            vside[b] = jnp.dot(v, sel_j, preferred_element_type=F32)

    sub = lax.broadcasted_iota(jnp.int32, (8, 2 * NQ), 0)

    def block_step(b, carry):
        x = ints[b]
        lhs = jnp.concatenate([x[:, i * 128 : (i + 1) * 128] for i in range(32)], axis=0)
        t = jnp.dot(lhs, wbd[b], preferred_element_type=F32)
        v = vside[b]
        v_lo = jnp.concatenate([v[:8], v[:8]], axis=1)
        v_hi = jnp.concatenate([v[8:], v[8:]], axis=1)
        tiles = [t[16 * p : 16 * p + 8] * v_lo + t[16 * p + 8 : 16 * p + 16] * v_hi for p in range(32)]
        for bit in range(3):
            mask = (sub & (1 << bit)) == 0
            tiles = [
                jnp.where(mask, a, c) + pltpu.roll(jnp.where(mask, c, a), 1 << bit, 0)
                for a, c in zip(tiles[0::2], tiles[1::2])
            ]
        for r in range(NX):
            for lo in range(2):
                parts[pl.ds((r * PQ + lo * 8) * NB + b, 8, stride=NB), :] = tiles[r][:, lo * NQ : (lo + 1) * NQ]
        return carry

    def remote(src, dst, send, recv, to):
        return pltpu.make_async_remote_copy(
            src_ref=src, dst_ref=dst, send_sem=send, recv_sem=recv, device_id=to, device_id_type=MESH
        )

    parts4 = parts.reshape(NX, PQ, NB, NQ)

    def span(g, k):
        n = NB // CHUNKS[g]
        return pl.ds(pl.multiple_of(k * n, n), n)

    def halves(g):
        p0, n = GROUPS[g]
        return pl.ds(p0, n // 2), pl.ds(p0 + n // 2, n // 2)

    def x_copy(g, i, k):
        at = span(g, k)
        lo, hi = halves(g)
        src, dst, to = {
            0: ((x_opp, lo, at), rxo.at[lo, at], right_x),
            1: ((x_opp, hi, at), rxo.at[hi, at], left_x),
            2: ((x_r, hi, at), rxn.at[0, hi, at], right_x),
            3: ((x_l, lo, at), rxn.at[1, lo, at], left_x),
            4: ((x_r, lo, at), rxn.at[0, lo, at], right_x),
            5: ((x_l, hi, at), rxn.at[1, hi, at], left_x),
        }[i]
        return remote(parts4.at[src], dst, xs.at[g, i, k], xr.at[g, i, k], to)

    def x_first(g, k):
        for i in range(4):
            x_copy(g, i, k).start()

    def x_second(g, k):
        at = span(g, k)
        lo, hi = halves(g)
        x_copy(g, 0, k).wait_recv()
        parts4[x_r, lo, at] += rxo[lo, at]
        x_copy(g, 4, k).start()
        x_copy(g, 1, k).wait_recv()
        parts4[x_l, hi, at] += rxo[hi, at]
        x_copy(g, 5, k).start()

    def core_copy(g):
        ps = pl.ds(*GROUPS[g])
        return remote(parts4.at[red, ps], coreacc.at[ps], cs.at[g], cr.at[g], other)

    def x_last(g):
        def one(k, carry):
            for i in (2, 3, 4, 5):
                x_copy(g, i, k).wait_recv()
            return carry

        lax.fori_loop(0, CHUNKS[g], one, 0)
        ps = pl.ds(*GROUPS[g])
        parts4[red, ps] += rxn[0, ps] + rxn[1, ps]
        core_copy(g).start()

    def compute(t):
        ints_copy(t).wait()
        sides(t)
        lax.fori_loop(0, CB, lambda i, carry: block_step(t * CB + i, carry), 0, unroll=CB)

    loads[2].wait()
    loads[3].wait()
    for k in range(1, NCH):
        ints_copy(k).start()
    compute(0)
    pl.semaphore_wait(barrier, len(peers))
    key_copy = remote(kown, koth, ks.at[0], kr.at[0], other)
    key_copy.start()
    x_first(0, 0)

    def chunk_step(t, carry):
        compute(t)
        x_first(0, t)

        @pl.when(t >= 2)
        def _():
            x_second(0, t - 2)

        @pl.when(t % 2 == 1)
        def _():
            x_first(1, t // 2)

        return carry

    lax.fori_loop(1, NCH, chunk_step, 0)

    def many(g, first, last):
        def one(k, carry):
            x_second(g, k)
            return carry

        lax.fori_loop(first, last, one, 0)

    key_copy.wait()
    lane = lax.broadcasted_iota(jnp.int32, (1, 2 * NB), 1)
    both_keys = jnp.where(lane < NB, kown[0:1, :], koth[0:1, :])
    row = lax.broadcasted_iota(jnp.int32, (NY * KEYS, 2 * NB), 0)
    ry, rz, rs = row // KEYS, (row // SLOTS) % NZ, row % SLOTS
    code = (((rz * NY) + ry) * 2 + core) * SLOTS + rs
    place = (code == both_keys).astype(F32).astype(BF)
    place2 = jnp.concatenate([place, place], axis=1)

    def y_halves(g):
        p0, n = GROUPS[g]
        return pl.ds(p0, n // 2), pl.ds(p0 + n // 2, n // 2)

    def y_copy(g, i):
        lo, hi = y_halves(g)
        src, dst, to = {
            0: ((lo, y_opp), ryo.at[lo], right_y),
            1: ((hi, y_opp), ryo.at[hi], left_y),
            2: ((hi, y_r), ryn.at[0, hi], right_y),
            3: ((lo, y_l), ryn.at[1, lo], left_y),
            4: ((lo, y_r), ryn.at[0, lo], right_y),
            5: ((hi, y_l), ryn.at[1, hi], left_y),
        }[i]
        return remote(dense.at[src], dst, ys.at[g, i], yr.at[g, i], to)

    def y_direct(g, h):
        ps = pl.ds(*GROUPS[g])
        yy = lax.rem(y + h, NY)
        return remote(dense.at[ps, yy], ryd.at[h - 1, ps], ys.at[g, h], yr.at[g, h], dev(z, yy, core, red))

    def y_copies(g, which):
        if RELAYED[g]:
            return [y_copy(g, i) for i in which]
        return [y_direct(g, h) for h in (2, 1, 3)]

    def y_second(g):
        lo, hi = y_halves(g)
        y_copy(g, 0).wait_recv()
        dense[lo, y_r] += ryo[lo]
        y_copy(g, 4).start()
        y_copy(g, 1).wait_recv()
        dense[hi, y_l] += ryo[hi]
        y_copy(g, 5).start()

    def densify(g):
        p0, n = GROUPS[g]
        core_copy(g).wait_recv()
        for p in range(p0, p0 + n, 2):
            own = jnp.concatenate([parts4[red, p], parts4[red, p + 1]], axis=1)
            oth = jnp.concatenate([coreacc[p], coreacc[p + 1]], axis=1)
            both = jnp.concatenate([own, oth], axis=0)
            high = both.astype(BF)
            rest = (both - high.astype(F32)).astype(BF)
            d = jnp.dot(place2, jnp.concatenate([high, rest], axis=0), preferred_element_type=F32)
            dense[p] = d[:, :NQ].reshape(NY, KEYS, NQ)
            dense[p + 1] = d[:, NQ:].reshape(NY, KEYS, NQ)
        for c in y_copies(g, range(4)):
            c.start()

    def z_rows(g):
        p0, n = GROUPS[g]
        return pl.ds(p0 * SLOTS, n * SLOTS)

    def z_copy(g, h):
        zz = lax.rem(z + h, NZ)
        at = z_rows(g)
        return remote(zbuf.at[zz, at], zrecv.at[z, at], zs.at[g, h], zr.at[g, z], dev(zz, y, core, red))

    def z_wait(g, h):
        zz = lax.rem(z + h, NZ)
        at = z_rows(g)
        remote(zbuf.at[zz, at], zrecv.at[zz, at], zs.at[g, h], zr.at[g, zz], other).wait_recv()

    zflat = zbuf.reshape(NZ * SLOTS * PQ, NQ)

    def y_last(g):
        p0, n = GROUPS[g]
        for c in y_copies(g, range(2, 6)):
            c.wait_recv()
        for i in range(n):
            p = p0 + i
            total = dense[p, y]
            if RELAYED[g]:
                total = total + (ryn[0, p] + ryn[1, p])
            else:
                total = total + (ryd[0, p] + ryd[1, p] + ryd[2, p])
            for zz in range(NZ):
                zflat[pl.ds(zz * SLOTS * PQ + p0 * SLOTS + i, SLOTS, stride=n), :] = total[zz * SLOTS : (zz + 1) * SLOTS]
        for h in (4, 3, 5, 2, 6, 1, 7):
            z_copy(g, h).start()

    def z_last(g):
        p0, n = GROUPS[g]
        for h in range(1, NZ):
            z_wait(g, h)
        at = z_rows(g)
        total = zbuf[z, at]
        for h in range(1, NZ):
            total = total + zrecv[lax.rem(z + h, NZ), at]
        lo, i0 = p0 // 8, p0 % 8
        for slot in range(SLOTS):
            outf[pl.ds(slot * PQ + 2 * i0 + lo, n, stride=2), :] = total[slot * n : (slot + 1) * n]

    def x_sent(g):
        def one(k, carry):
            for i in range(6):
                x_copy(g, i, k).wait_send()
            return carry

        lax.fori_loop(0, CHUNKS[g], one, 0)
        core_copy(g).wait_send()

    many(0, NCH - 2, NCH)
    x_first(2, 0)
    many(1, 0, CHUNKS[1])
    x_last(0)
    densify(0)
    x_second(2, 0)
    y_second(0)
    x_last(1)
    densify(1)
    x_last(2)
    densify(2)
    y_last(0)
    x_sent(0)
    x_sent(1)
    x_sent(2)
    y_last(1)
    y_last(2)
    z_last(0)
    z_last(1)
    z_last(2)
    out_ref[...] = outf[...].astype(BF).reshape(SLOTS, PQ, NQ)

    for g in range(NG):
        for c in y_copies(g, range(6)):
            c.wait_send()
        for h in range(1, NZ):
            z_copy(g, h).wait_send()


def shards(
    ints, block_pairs, block_dest, block_slot, occ_density, virt_density, isdf_cols, slab_cols
):
    hbm = pl.BlockSpec(memory_space=pl.ANY)
    vmem = pl.BlockSpec(memory_space=pltpu.VMEM)
    dma = pltpu.SemaphoreType.DMA
    pairs_t = block_pairs.T
    return pl.pallas_call(
        kernel,
        out_shape=jax.ShapeDtypeStruct((SLOTS, PQ, NQ), BF),
        in_specs=[hbm] * 8,
        out_specs=vmem,
        scratch_shapes=[
            pltpu.SMEM((2, NB), jnp.int32),
            pltpu.VMEM((2, NB), jnp.int32),
            pltpu.VMEM((1, NB), jnp.int32),
            pltpu.VMEM((1, NB), jnp.int32),
            pltpu.VMEM((1, NQ), jnp.int32),
            pltpu.VMEM((NB, LAM, BA * BA), BF),
            pltpu.VMEM((BA * BA, NAB), BF),
            pltpu.VMEM((LAM * BA, NAB), BF),
            pltpu.VMEM((NAB, BA, NCAND), BF),
            pltpu.VMEM((NB, BA * BA), F32),
            pltpu.VMEM((NB, LAM * BA), F32),
            pltpu.VMEM((CB * BA, 2 * BA), F32),
            pltpu.VMEM((CB * LAM, 2 * BA), F32),
            pltpu.VMEM((NB, 2 * BA, 2 * NQ), BF),
            pltpu.VMEM((NB, LAM, NQ), F32),
            pltpu.VMEM((NX * PQ * NB, NQ), F32),
            pltpu.VMEM((PQ, NB, NQ), F32),
            pltpu.VMEM((2, PQ, NB, NQ), F32),
            pltpu.VMEM((8, 128), jnp.int32),
            pltpu.VMEM((8, 128), jnp.int32),
            pltpu.VMEM((PQ, NB, NQ), F32),
            pltpu.VMEM((PQ, NY, KEYS, NQ), F32),
            pltpu.VMEM((PQ, KEYS, NQ), F32),
            pltpu.VMEM((2, PQ, KEYS, NQ), F32),
            pltpu.VMEM((NY - 1, PQ, KEYS, NQ), F32),
            pltpu.VMEM((NZ, SLOTS * PQ, NQ), F32),
            pltpu.VMEM((NZ, SLOTS * PQ, NQ), F32),
            pltpu.VMEM((SLOTS * PQ, NQ), F32),
            dma((5,)),
            dma((4,)),
            dma((NCH,)),
            dma((NG, 6, NCH)),
            dma((NG, 6, NCH)),
            dma((NG,)),
            dma((NG,)),
            dma((1,)),
            dma((1,)),
            dma((NG, 6)),
            dma((NG, 6)),
            dma((NG, NZ)),
            dma((NG, NZ)),
        ],
        compiler_params=pltpu.CompilerParams(
            collective_id=0, has_side_effects=True, vmem_limit_bytes=56 * 1024 * 1024
        ),
        cost_estimate=pl.CostEstimate(flops=3_000_000_000, bytes_accessed=14_000_000, transcendentals=0),
    )(
        ints,
        pairs_t,
        block_dest.reshape(1, NB),
        block_slot.reshape(1, NB),
        slab_cols.reshape(1, NQ),
        occ_density.transpose(1, 2, 0).reshape(BA * BA, NAB),
        virt_density.transpose(1, 2, 0).reshape(BA * BA, NAB),
        isdf_cols,
    )


def solution(mesh):
    return jax.shard_map(
        shards,
        mesh=mesh,
        in_specs=(
            P("pair", "red", None),
            P("pair", None),
            P("pair", None),
            P("pair"),
            P(),
            P(),
            P(),
            P(),
        ),
        out_specs=P("pair", "red", None),
        check_vma=False,
    )
```

```python
import functools

import jax
import jax.numpy as jnp
from jax import lax
from jax.experimental import pallas as pl
from jax.experimental.pallas import tpu as pltpu
from jax.sharding import PartitionSpec as P

MESH = pl.DeviceIdType.MESH
BF, F32 = jnp.bfloat16, jnp.float32

NB = 64
LAM = 16
BA = 64
NAB = 96
NQ = 128
NCAND = 256
PQ = 16
NX, NY, NZ = 4, 4, 8
SLOTS = 4
CB = 8
NCH = NB // CB
GROUPS = ((0, 8), (8, 4), (12, 4))
NG = len(GROUPS)
RELAYED = (True, False, False)
CHUNKS = (8, 4, 1)
KEYS = NZ * SLOTS


def kernel(
    ints_hbm, pairs_hbm, dest_hbm, slot_hbm, slab_hbm, occ_hbm, virt_hbm, isdf_hbm,
    out_ref,
    pairs_smem, pairs_ref, dest_ref, slot_ref, slab_ref, ints, occ_t, virt_t, isdf, dflat, vflat, dens, vdens, wbd, vside,
    parts, rxo, rxn, kown, koth, coreacc, dense, ryo, ryn, ryd, zbuf, zrecv, outf,
    small_sem, load_sem, ints_sem, xs, xr, xl, cs, cr, ks, kr, ys, yr, zs, zr,
):
    pair = lax.axis_index("pair")
    red = lax.axis_index("red")
    core = lax.rem(pair, 2)
    y = lax.rem(pair // 2, NY)
    z = pair // (2 * NY)

    def dev(zz, yy, cc, rr):
        return ((zz * NY + yy) * 2 + cc, rr)

    y_opp, y_r, y_l = lax.rem(y + 2, NY), lax.rem(y + 1, NY), lax.rem(y + 3, NY)
    x_opp, x_r, x_l = lax.rem(red + 2, NX), lax.rem(red + 1, NX), lax.rem(red + 3, NX)
    right_x, left_x = dev(z, y, core, x_r), dev(z, y, core, x_l)
    right_y, left_y = dev(z, y_r, core, red), dev(z, y_l, core, red)
    other = dev(z, y, 1 - core, red)

    small = [
        pltpu.make_async_copy(src, dst, small_sem.at[i])
        for i, (src, dst) in enumerate(
            (
                (pairs_hbm, pairs_ref),
                (slab_hbm, slab_ref),
                (dest_hbm, dest_ref),
                (slot_hbm, slot_ref),
                (pairs_hbm, pairs_smem),
            )
        )
    ]
    for c in small:
        c.start()
    half = NAB // 2
    loads = [
        pltpu.make_async_copy(virt_hbm.at[pl.ds(red * (LAM * BA), LAM * BA)], virt_t, load_sem.at[0]),
        pltpu.make_async_copy(occ_hbm, occ_t, load_sem.at[1]),
        pltpu.make_async_copy(isdf_hbm.at[pl.ds(0, half)], isdf.at[pl.ds(0, half)], load_sem.at[2]),
        pltpu.make_async_copy(isdf_hbm.at[pl.ds(half, half)], isdf.at[pl.ds(half, half)], load_sem.at[3]),
    ]
    for c in loads:
        c.start()

    def ints_copy(k):
        return pltpu.make_async_copy(
            ints_hbm.at[pl.ds(k * CB, CB)], ints.at[pl.ds(k * CB, CB)], ints_sem.at[k]
        )

    ints_copy(0).start()

    barrier = pltpu.get_barrier_semaphore()
    peers = [right_x, left_x, right_y, left_y, dev(z, y_opp, core, red), other]
    peers += [dev(lax.rem(z + h, NZ), y, core, red) for h in range(1, NZ)]
    for d in peers:
        pl.semaphore_signal(barrier, inc=1, device_id=d, device_id_type=MESH)

    for c in small:
        c.wait()
    pick = (lax.broadcasted_iota(jnp.int32, (NCAND, NQ), 0) == slab_ref[...]).astype(F32).astype(BF)

    def one_hot_rows(row):
        wide = jnp.concatenate([pairs_ref[row : row + 1, :], jnp.full((1, 128 - NB), -1, jnp.int32)], axis=1)
        t = (lax.broadcasted_iota(jnp.int32, (128, 128), 0) == wide).astype(F32)
        return jnp.transpose(t)[:NB, :NAB].astype(BF)

    hot_i, hot_j = one_hot_rows(0), one_hot_rows(1)
    keys = dest_ref[...] * SLOTS + slot_ref[...]
    kown[...] = jnp.broadcast_to(jnp.concatenate([keys, keys], axis=1), (8, 128))

    low = lax.broadcasted_iota(jnp.int32, (CB, 128), 1) < BA

    def gathered(hot, src, dst):
        for at in range(0, dst.shape[1], 512):
            dst[:, at : at + 512] = lax.dot_general(
                hot, src[at : at + 512, :], (((1,), (1,)), ((), ())), preferred_element_type=F32
            )

    def turned(flat, t, dst, count):
        at = pl.ds(pl.multiple_of(t * CB, CB), CB)
        for m in range(0, count, 2):
            both = flat[at, m * BA : (m + 2) * BA]
            back = pltpu.roll(both, BA, 1)
            dst[pl.ds(m, CB, stride=count), :] = jnp.where(low, both, back)
            dst[pl.ds(m + 1, CB, stride=count), :] = jnp.where(low, back, both)

    loads[0].wait()
    gathered(hot_j, virt_t, vflat)
    loads[1].wait()
    gathered(hot_i, occ_t, dflat)

    top = lax.broadcasted_iota(jnp.int32, (2 * BA, NQ), 0) < BA

    def sides(t):
        turned(vflat, t, vdens, LAM)
        turned(dflat, t, dens, BA)
        ids = [(pairs_smem[0, t * CB + i], pairs_smem[1, t * CB + i]) for i in range(CB)]
        cols = jnp.concatenate([isdf[a] for both in ids for a in both], axis=0)
        sel = jnp.dot(cols, pick, preferred_element_type=F32).astype(BF)
        for i in range(CB):
            b = t * CB + i
            sel_i, sel_j = sel[2 * i * BA : (2 * i + 1) * BA], sel[(2 * i + 1) * BA : (2 * i + 2) * BA]
            d = dens[i * BA : (i + 1) * BA, :].astype(BF)
            occ = lax.dot_general(d, sel_i, (((0,), (0,)), ((), ())), preferred_element_type=F32)
            wbd[b] = jnp.concatenate([jnp.where(top, occ, 0.0), jnp.where(top, 0.0, occ)], axis=1).astype(BF)
            v = vdens[i * LAM : (i + 1) * LAM, :BA].astype(BF)
            vside[b] = jnp.dot(v, sel_j, preferred_element_type=F32)

    sub = lax.broadcasted_iota(jnp.int32, (8, 2 * NQ), 0)

    def block_step(b, carry):
        x = ints[b]
        lhs = jnp.concatenate([x[:, i * 128 : (i + 1) * 128] for i in range(32)], axis=0)
        t = jnp.dot(lhs, wbd[b], preferred_element_type=F32)
        v = vside[b]
        v_lo = jnp.concatenate([v[:8], v[:8]], axis=1)
        v_hi = jnp.concatenate([v[8:], v[8:]], axis=1)
        tiles = [t[16 * p : 16 * p + 8] * v_lo + t[16 * p + 8 : 16 * p + 16] * v_hi for p in range(32)]
        for bit in range(3):
            mask = (sub & (1 << bit)) == 0
            tiles = [
                jnp.where(mask, a, c) + pltpu.roll(jnp.where(mask, c, a), 1 << bit, 0)
                for a, c in zip(tiles[0::2], tiles[1::2])
            ]
        for r in range(NX):
            for lo in range(2):
                parts[pl.ds((r * PQ + lo * 8) * NB + b, 8, stride=NB), :] = tiles[r][:, lo * NQ : (lo + 1) * NQ]
        return carry

    def remote(src, dst, send, recv, to):
        return pltpu.make_async_remote_copy(
            src_ref=src, dst_ref=dst, send_sem=send, recv_sem=recv, device_id=to, device_id_type=MESH
        )

    parts4 = parts.reshape(NX, PQ, NB, NQ)

    def span(g, k):
        n = NB // CHUNKS[g]
        return pl.ds(pl.multiple_of(k * n, n), n)

    def halves(g):
        p0, n = GROUPS[g]
        return pl.ds(p0, n // 2), pl.ds(p0 + n // 2, n // 2)

    def x_copy(g, i, k):
        at = span(g, k)
        lo, hi = halves(g)
        src, dst, to = {
            0: ((x_opp, lo, at), rxo.at[lo, at], right_x),
            1: ((x_opp, hi, at), rxo.at[hi, at], left_x),
            2: ((x_r, hi, at), rxn.at[0, hi, at], right_x),
            3: ((x_l, lo, at), rxn.at[1, lo, at], left_x),
            4: ((x_r, lo, at), rxn.at[0, lo, at], right_x),
            5: ((x_l, hi, at), rxn.at[1, hi, at], left_x),
        }[i]
        recv = xr.at[i * sum(CHUNKS) + sum(CHUNKS[:g]) + k] if i < 2 else xl.at[g]
        return remote(parts4.at[src], dst, xs.at[g], recv, to)

    def x_first(g, k):
        for i in range(4):
            x_copy(g, i, k).start()

    def x_second(g, k):
        at = span(g, k)
        lo, hi = halves(g)
        x_copy(g, 0, k).wait_recv()
        parts4[x_r, lo, at] += rxo[lo, at]
        x_copy(g, 4, k).start()
        x_copy(g, 1, k).wait_recv()
        parts4[x_l, hi, at] += rxo[hi, at]
        x_copy(g, 5, k).start()

    def core_copy(g):
        ps = pl.ds(*GROUPS[g])
        return remote(parts4.at[red, ps], coreacc.at[ps], cs.at[g], cr.at[g], other)

    def x_last(g):
        late = rxn.at[:, pl.ds(*GROUPS[g])]
        remote(late, late, xs.at[g], xl.at[g], other).wait_recv()
        ps = pl.ds(*GROUPS[g])
        parts4[red, ps] += rxn[0, ps] + rxn[1, ps]
        core_copy(g).start()

    def compute(t):
        ints_copy(t).wait()
        sides(t)
        lax.fori_loop(0, CB, lambda i, carry: block_step(t * CB + i, carry), 0, unroll=CB)

    loads[2].wait()
    loads[3].wait()
    for k in range(1, NCH):
        ints_copy(k).start()
    compute(0)
    pl.semaphore_wait(barrier, len(peers))
    key_copy = remote(kown, koth, ks.at[0], kr.at[0], other)
    key_copy.start()
    x_first(0, 0)

    def chunk_step(t, carry):
        compute(t)
        x_first(0, t)

        @pl.when(t >= 2)
        def _():
            x_second(0, t - 2)

        @pl.when(t % 2 == 1)
        def _():
            x_first(1, t // 2)

        return carry

    lax.fori_loop(1, NCH, chunk_step, 0)

    def many(g, first, last):
        def one(k, carry):
            x_second(g, k)
            return carry

        lax.fori_loop(first, last, one, 0)

    key_copy.wait()
    lane = lax.broadcasted_iota(jnp.int32, (1, 2 * NB), 1)
    both_keys = jnp.where(lane < NB, kown[0:1, :], koth[0:1, :])
    row = lax.broadcasted_iota(jnp.int32, (NY * KEYS, 2 * NB), 0)
    ry, rz, rs = row // KEYS, (row // SLOTS) % NZ, row % SLOTS
    code = (((rz * NY) + ry) * 2 + core) * SLOTS + rs
    place = (code == both_keys).astype(F32).astype(BF)
    place2 = jnp.concatenate([place, place], axis=1)

    def y_halves(g):
        p0, n = GROUPS[g]
        return pl.ds(p0, n // 2), pl.ds(p0 + n // 2, n // 2)

    def y_copy(g, i):
        lo, hi = y_halves(g)
        src, dst, to = {
            0: ((lo, y_opp), ryo.at[lo], right_y),
            1: ((hi, y_opp), ryo.at[hi], left_y),
            2: ((hi, y_r), ryn.at[0, hi], right_y),
            3: ((lo, y_l), ryn.at[1, lo], left_y),
            4: ((lo, y_r), ryn.at[0, lo], right_y),
            5: ((hi, y_l), ryn.at[1, hi], left_y),
        }[i]
        return remote(dense.at[src], dst, ys.at[g], yr.at[g, i if i < 2 else 2], to)

    def y_direct(g, h):
        ps = pl.ds(*GROUPS[g])
        yy = lax.rem(y + h, NY)
        return remote(dense.at[ps, yy], ryd.at[h - 1, ps], ys.at[g], yr.at[g, 2], dev(z, yy, core, red))

    def y_copies(g, which):
        if RELAYED[g]:
            return [y_copy(g, i) for i in which]
        return [y_direct(g, h) for h in (2, 1, 3)]

    def y_second(g):
        lo, hi = y_halves(g)
        y_copy(g, 0).wait_recv()
        dense[lo, y_r] += ryo[lo]
        y_copy(g, 4).start()
        y_copy(g, 1).wait_recv()
        dense[hi, y_l] += ryo[hi]
        y_copy(g, 5).start()

    def densify(g):
        p0, n = GROUPS[g]
        core_copy(g).wait_recv()
        for p in range(p0, p0 + n, 2):
            own = jnp.concatenate([parts4[red, p], parts4[red, p + 1]], axis=1)
            oth = jnp.concatenate([coreacc[p], coreacc[p + 1]], axis=1)
            both = jnp.concatenate([own, oth], axis=0)
            high = both.astype(BF)
            rest = (both - high.astype(F32)).astype(BF)
            d = jnp.dot(place2, jnp.concatenate([high, rest], axis=0), preferred_element_type=F32)
            dense[p] = d[:, :NQ].reshape(NY, KEYS, NQ)
            dense[p + 1] = d[:, NQ:].reshape(NY, KEYS, NQ)
        for c in y_copies(g, range(4)):
            c.start()

    def z_rows(g):
        p0, n = GROUPS[g]
        return pl.ds(p0 * SLOTS, n * SLOTS)

    def z_copy(g, h):
        zz = lax.rem(z + h, NZ)
        at = z_rows(g)
        return remote(zbuf.at[zz, at], zrecv.at[z, at], zs.at[g], zr.at[g], dev(zz, y, core, red))

    def z_all(g):
        every = zrecv.at[pl.ds(0, NZ - 1), z_rows(g)]
        return remote(every, every, zs.at[g], zr.at[g], other)

    zflat = zbuf.reshape(NZ * SLOTS * PQ, NQ)

    def y_last(g):
        p0, n = GROUPS[g]
        late = (ryn if RELAYED[g] else ryd).at[:, pl.ds(p0, n)]
        remote(late, late, ys.at[g], yr.at[g, 2], other).wait_recv()
        for i in range(n):
            p = p0 + i
            total = dense[p, y]
            if RELAYED[g]:
                total = total + (ryn[0, p] + ryn[1, p])
            else:
                total = total + (ryd[0, p] + ryd[1, p] + ryd[2, p])
            for zz in range(NZ):
                zflat[pl.ds(zz * SLOTS * PQ + p0 * SLOTS + i, SLOTS, stride=n), :] = total[zz * SLOTS : (zz + 1) * SLOTS]
        for h in (4, 3, 5, 2, 6, 1, 7):
            z_copy(g, h).start()

    def z_last(g):
        p0, n = GROUPS[g]
        z_all(g).wait_recv()
        at = z_rows(g)
        total = zbuf[z, at]
        for h in range(1, NZ):
            total = total + zrecv[lax.rem(z + h, NZ), at]
        lo, i0 = p0 // 8, p0 % 8
        for slot in range(SLOTS):
            outf[pl.ds(slot * PQ + 2 * i0 + lo, n, stride=2), :] = total[slot * n : (slot + 1) * n]

    def x_sent(g):
        sent = parts4.at[pl.ds(0, 3), pl.ds(*GROUPS[g])]
        remote(sent, sent, xs.at[g], xl.at[g], other).wait_send()
        core_copy(g).wait_send()

    many(0, NCH - 2, NCH)
    x_first(2, 0)
    many(1, 0, CHUNKS[1])
    x_last(0)
    densify(0)
    x_second(2, 0)
    y_second(0)
    x_last(1)
    densify(1)
    x_last(2)
    densify(2)
    y_last(0)
    x_sent(0)
    x_sent(1)
    x_sent(2)
    y_last(1)
    y_last(2)
    z_last(0)
    z_last(1)
    z_last(2)
    out_ref[...] = outf[...].astype(BF).reshape(SLOTS, PQ, NQ)

    for g in range(NG):
        sent = dense.at[pl.ds(*GROUPS[g]), pl.ds(0, 3)]
        remote(sent, sent, ys.at[g], yr.at[g, 2], other).wait_send()
        z_all(g).wait_send()


def shards(
    ints, block_pairs, block_dest, block_slot, occ_density, virt_density, isdf_cols, slab_cols
):
    hbm = pl.BlockSpec(memory_space=pl.ANY)
    vmem = pl.BlockSpec(memory_space=pltpu.VMEM)
    dma = pltpu.SemaphoreType.DMA
    pairs_t = block_pairs.T
    return pl.pallas_call(
        kernel,
        out_shape=jax.ShapeDtypeStruct((SLOTS, PQ, NQ), BF),
        in_specs=[hbm] * 8,
        out_specs=vmem,
        scratch_shapes=[
            pltpu.SMEM((2, NB), jnp.int32),
            pltpu.VMEM((2, NB), jnp.int32),
            pltpu.VMEM((1, NB), jnp.int32),
            pltpu.VMEM((1, NB), jnp.int32),
            pltpu.VMEM((1, NQ), jnp.int32),
            pltpu.VMEM((NB, LAM, BA * BA), BF),
            pltpu.VMEM((BA * BA, NAB), BF),
            pltpu.VMEM((LAM * BA, NAB), BF),
            pltpu.VMEM((NAB, BA, NCAND), BF),
            pltpu.VMEM((NB, BA * BA), F32),
            pltpu.VMEM((NB, LAM * BA), F32),
            pltpu.VMEM((CB * BA, 2 * BA), F32),
            pltpu.VMEM((CB * LAM, 2 * BA), F32),
            pltpu.VMEM((NB, 2 * BA, 2 * NQ), BF),
            pltpu.VMEM((NB, LAM, NQ), F32),
            pltpu.VMEM((NX * PQ * NB, NQ), F32),
            pltpu.VMEM((PQ, NB, NQ), F32),
            pltpu.VMEM((2, PQ, NB, NQ), F32),
            pltpu.VMEM((8, 128), jnp.int32),
            pltpu.VMEM((8, 128), jnp.int32),
            pltpu.VMEM((PQ, NB, NQ), F32),
            pltpu.VMEM((PQ, NY, KEYS, NQ), F32),
            pltpu.VMEM((PQ, KEYS, NQ), F32),
            pltpu.VMEM((2, PQ, KEYS, NQ), F32),
            pltpu.VMEM((NY - 1, PQ, KEYS, NQ), F32),
            pltpu.VMEM((NZ, SLOTS * PQ, NQ), F32),
            pltpu.VMEM((NZ, SLOTS * PQ, NQ), F32),
            pltpu.VMEM((SLOTS * PQ, NQ), F32),
            dma((5,)),
            dma((4,)),
            dma((NCH,)),
            dma((NG,)),
            dma((2 * sum(CHUNKS),)),
            dma((NG,)),
            dma((NG,)),
            dma((NG,)),
            dma((1,)),
            dma((1,)),
            dma((NG,)),
            dma((NG, 3)),
            dma((NG,)),
            dma((NG,)),
        ],
        compiler_params=pltpu.CompilerParams(
            collective_id=0, has_side_effects=True, vmem_limit_bytes=56 * 1024 * 1024
        ),
        cost_estimate=pl.CostEstimate(flops=3_000_000_000, bytes_accessed=14_000_000, transcendentals=0),
    )(
        ints,
        pairs_t,
        block_dest.reshape(1, NB),
        block_slot.reshape(1, NB),
        slab_cols.reshape(1, NQ),
        occ_density.transpose(1, 2, 0).reshape(BA * BA, NAB),
        virt_density.transpose(1, 2, 0).reshape(BA * BA, NAB),
        isdf_cols,
    )


def solution(mesh):
    return jax.shard_map(
        shards,
        mesh=mesh,
        in_specs=(
            P("pair", "red", None),
            P("pair", None),
            P("pair", None),
            P("pair"),
            P(),
            P(),
            P(),
            P(),
        ),
        out_specs=P("pair", "red", None),
        check_vma=False,
    )
```

```python
import functools

import jax
import jax.numpy as jnp
from jax import lax
from jax.experimental import pallas as pl
from jax.experimental.pallas import tpu as pltpu
from jax.sharding import PartitionSpec as P

MESH = pl.DeviceIdType.MESH
BF, F32 = jnp.bfloat16, jnp.float32

NB = 64
LAM = 16
BA = 64
NAB = 96
NQ = 128
NCAND = 256
PQ = 16
NX, NY, NZ = 4, 4, 8
SLOTS = 4
CB = 8
NCH = NB // CB
GROUPS = ((0, 8), (8, 4), (12, 4))
NG = len(GROUPS)
RELAYED = (True, False, False)
CHUNKS = (8, 4, 1)
KEYS = NZ * SLOTS


def kernel(
    ints_hbm, pairs_hbm, dest_hbm, slot_hbm, slab_hbm, occ_hbm, virt_hbm, isdf_hbm,
    out_ref,
    pairs_smem, pairs_ref, dest_ref, slot_ref, slab_ref, ints, occ_t, virt_t, isdf, dflat, vflat, dens, vdens, wbd, vside,
    parts, rxo, rxn, kown, koth, coreacc, dense, ryo, ryn, ryd, zbuf, zrecv, outf,
    small_sem, load_sem, ints_sem, xs, xr, xl, cs, cr, ks, kr, ys, yr, zs, zr,
):
    pair = lax.axis_index("pair")
    red = lax.axis_index("red")
    core = lax.rem(pair, 2)
    y = lax.rem(pair // 2, NY)
    z = pair // (2 * NY)

    def dev(zz, yy, cc, rr):
        return ((zz * NY + yy) * 2 + cc, rr)

    y_opp, y_r, y_l = lax.rem(y + 2, NY), lax.rem(y + 1, NY), lax.rem(y + 3, NY)
    x_opp, x_r, x_l = lax.rem(red + 2, NX), lax.rem(red + 1, NX), lax.rem(red + 3, NX)
    right_x, left_x = dev(z, y, core, x_r), dev(z, y, core, x_l)
    right_y, left_y = dev(z, y_r, core, red), dev(z, y_l, core, red)
    other = dev(z, y, 1 - core, red)

    small = [
        pltpu.make_async_copy(src, dst, small_sem.at[i])
        for i, (src, dst) in enumerate(
            (
                (pairs_hbm, pairs_ref),
                (slab_hbm, slab_ref),
                (dest_hbm, dest_ref),
                (slot_hbm, slot_ref),
                (pairs_hbm, pairs_smem),
            )
        )
    ]
    for c in small:
        c.start()
    half = NAB // 2
    loads = [
        pltpu.make_async_copy(virt_hbm.at[pl.ds(red * (LAM * BA), LAM * BA)], virt_t, load_sem.at[0]),
        pltpu.make_async_copy(occ_hbm, occ_t, load_sem.at[1]),
        pltpu.make_async_copy(isdf_hbm.at[pl.ds(0, half)], isdf.at[pl.ds(0, half)], load_sem.at[2]),
        pltpu.make_async_copy(isdf_hbm.at[pl.ds(half, half)], isdf.at[pl.ds(half, half)], load_sem.at[3]),
    ]
    for c in loads:
        c.start()

    def ints_copy(k):
        return pltpu.make_async_copy(
            ints_hbm.at[pl.ds(k * CB, CB)], ints.at[pl.ds(k * CB, CB)], ints_sem.at[k]
        )

    ints_copy(0).start()

    barrier = pltpu.get_barrier_semaphore()
    peers = [right_x, left_x, right_y, left_y, dev(z, y_opp, core, red), other]
    peers += [dev(lax.rem(z + h, NZ), y, core, red) for h in range(1, NZ)]
    for d in peers:
        pl.semaphore_signal(barrier, inc=1, device_id=d, device_id_type=MESH)

    for c in small:
        c.wait()
    pick = (lax.broadcasted_iota(jnp.int32, (NCAND, NQ), 0) == slab_ref[...]).astype(F32).astype(BF)

    def one_hot_rows(row):
        wide = jnp.concatenate([pairs_ref[row : row + 1, :], jnp.full((1, 128 - NB), -1, jnp.int32)], axis=1)
        t = (lax.broadcasted_iota(jnp.int32, (128, 128), 0) == wide).astype(F32)
        return jnp.transpose(t)[:NB, :NAB].astype(BF)

    hot_i, hot_j = one_hot_rows(0), one_hot_rows(1)
    keys = dest_ref[...] * SLOTS + slot_ref[...]
    kown[...] = jnp.broadcast_to(jnp.concatenate([keys, keys], axis=1), (8, 128))

    low = lax.broadcasted_iota(jnp.int32, (CB, 128), 1) < BA

    def gathered(hot, src, dst):
        for at in range(0, dst.shape[1], 512):
            dst[:, at : at + 512] = lax.dot_general(
                hot, src[at : at + 512, :], (((1,), (1,)), ((), ())), preferred_element_type=F32
            )

    def turned(flat, t, dst, count):
        at = pl.ds(pl.multiple_of(t * CB, CB), CB)
        for m in range(0, count, 2):
            both = flat[at, m * BA : (m + 2) * BA]
            back = pltpu.roll(both, BA, 1)
            dst[pl.ds(m, CB, stride=count), :] = jnp.where(low, both, back)
            dst[pl.ds(m + 1, CB, stride=count), :] = jnp.where(low, back, both)

    loads[0].wait()
    gathered(hot_j, virt_t, vflat)
    loads[1].wait()
    gathered(hot_i, occ_t, dflat)

    top = lax.broadcasted_iota(jnp.int32, (2 * BA, NQ), 0) < BA

    def sides(t):
        turned(vflat, t, vdens, LAM)
        turned(dflat, t, dens, BA)
        ids = [(pairs_smem[0, t * CB + i], pairs_smem[1, t * CB + i]) for i in range(CB)]
        cols = jnp.concatenate([isdf[a] for both in ids for a in both], axis=0)
        sel = jnp.dot(cols, pick, preferred_element_type=F32).astype(BF)
        for i in range(CB):
            b = t * CB + i
            sel_i, sel_j = sel[2 * i * BA : (2 * i + 1) * BA], sel[(2 * i + 1) * BA : (2 * i + 2) * BA]
            d = dens[i * BA : (i + 1) * BA, :].astype(BF)
            occ = lax.dot_general(d, sel_i, (((0,), (0,)), ((), ())), preferred_element_type=F32)
            wbd[b] = jnp.concatenate([jnp.where(top, occ, 0.0), jnp.where(top, 0.0, occ)], axis=1).astype(BF)
            v = vdens[i * LAM : (i + 1) * LAM, :BA].astype(BF)
            vside[b] = jnp.dot(v, sel_j, preferred_element_type=F32)

    sub = lax.broadcasted_iota(jnp.int32, (8, 2 * NQ), 0)

    def block_step(b, carry):
        x = ints[b]
        lhs = jnp.concatenate([x[:, i * 128 : (i + 1) * 128] for i in range(32)], axis=0)
        t = jnp.dot(lhs, wbd[b], preferred_element_type=F32)
        v = vside[b]
        v_lo = jnp.concatenate([v[:8], v[:8]], axis=1)
        v_hi = jnp.concatenate([v[8:], v[8:]], axis=1)
        tiles = [t[16 * p : 16 * p + 8] * v_lo + t[16 * p + 8 : 16 * p + 16] * v_hi for p in range(32)]
        for bit in range(3):
            mask = (sub & (1 << bit)) == 0
            tiles = [
                jnp.where(mask, a, c) + pltpu.roll(jnp.where(mask, c, a), 1 << bit, 0)
                for a, c in zip(tiles[0::2], tiles[1::2])
            ]
        for r in range(NX):
            for lo in range(2):
                parts[pl.ds((r * PQ + lo * 8) * NB + b, 8, stride=NB), :] = tiles[r][:, lo * NQ : (lo + 1) * NQ]
        return carry

    def remote(src, dst, send, recv, to):
        return pltpu.make_async_remote_copy(
            src_ref=src, dst_ref=dst, send_sem=send, recv_sem=recv, device_id=to, device_id_type=MESH
        )

    parts4 = parts.reshape(NX, PQ, NB, NQ)

    def span(g, k):
        n = NB // CHUNKS[g]
        return pl.ds(pl.multiple_of(k * n, n), n)

    def halves(g):
        p0, n = GROUPS[g]
        return pl.ds(p0, n // 2), pl.ds(p0 + n // 2, n // 2)

    def x_copy(g, i, k):
        at = span(g, k)
        lo, hi = halves(g)
        src, dst, to = {
            0: ((x_opp, lo, at), rxo.at[lo, at], right_x),
            1: ((x_opp, hi, at), rxo.at[hi, at], left_x),
            2: ((x_r, hi, at), rxn.at[0, hi, at], right_x),
            3: ((x_l, lo, at), rxn.at[1, lo, at], left_x),
            4: ((x_r, lo, at), rxn.at[0, lo, at], right_x),
            5: ((x_l, hi, at), rxn.at[1, hi, at], left_x),
        }[i]
        recv = xr.at[i * sum(CHUNKS) + sum(CHUNKS[:g]) + k] if i < 2 else xl.at[g]
        return remote(parts4.at[src], dst, xs.at[g], recv, to)

    def x_first(g, k):
        for i in range(4):
            x_copy(g, i, k).start()

    def x_second(g, k):
        at = span(g, k)
        lo, hi = halves(g)
        x_copy(g, 0, k).wait_recv()
        parts4[x_r, lo, at] += rxo[lo, at]
        x_copy(g, 4, k).start()
        x_copy(g, 1, k).wait_recv()
        parts4[x_l, hi, at] += rxo[hi, at]
        x_copy(g, 5, k).start()

    def core_copy(g):
        ps = pl.ds(*GROUPS[g])
        return remote(parts4.at[red, ps], coreacc.at[ps], cs.at[g], cr.at[g], other)

    def x_last(g):
        late = rxn.at[:, pl.ds(*GROUPS[g])]
        remote(late, late, xs.at[g], xl.at[g], other).wait_recv()
        ps = pl.ds(*GROUPS[g])
        parts4[red, ps] += rxn[0, ps] + rxn[1, ps]
        core_copy(g).start()

    def compute(t):
        ints_copy(t).wait()
        sides(t)
        lax.fori_loop(0, CB, lambda i, carry: block_step(t * CB + i, carry), 0, unroll=CB)

    loads[2].wait()
    loads[3].wait()
    for k in range(1, NCH):
        ints_copy(k).start()
    compute(0)
    pl.semaphore_wait(barrier, len(peers))
    key_copy = remote(kown, koth, ks.at[0], kr.at[0], other)
    key_copy.start()
    x_first(0, 0)

    def chunk_step(t, carry):
        compute(t)
        x_first(0, t)

        @pl.when(t >= 3)
        def _():
            x_second(0, t - 3)

        @pl.when(t % 2 == 1)
        def _():
            x_first(1, t // 2)

        return carry

    lax.fori_loop(1, NCH, chunk_step, 0)

    def many(g, first, last):
        def one(k, carry):
            x_second(g, k)
            return carry

        lax.fori_loop(first, last, one, 0)

    key_copy.wait()
    lane = lax.broadcasted_iota(jnp.int32, (1, 2 * NB), 1)
    both_keys = jnp.where(lane < NB, kown[0:1, :], koth[0:1, :])
    row = lax.broadcasted_iota(jnp.int32, (NY * KEYS, 2 * NB), 0)
    ry, rz, rs = row // KEYS, (row // SLOTS) % NZ, row % SLOTS
    code = (((rz * NY) + ry) * 2 + core) * SLOTS + rs
    place = (code == both_keys).astype(F32).astype(BF)
    place2 = jnp.concatenate([place, place], axis=1)

    def y_halves(g):
        p0, n = GROUPS[g]
        return pl.ds(p0, n // 2), pl.ds(p0 + n // 2, n // 2)

    def y_copy(g, i):
        lo, hi = y_halves(g)
        src, dst, to = {
            0: ((lo, y_opp), ryo.at[lo], right_y),
            1: ((hi, y_opp), ryo.at[hi], left_y),
            2: ((hi, y_r), ryn.at[0, hi], right_y),
            3: ((lo, y_l), ryn.at[1, lo], left_y),
            4: ((lo, y_r), ryn.at[0, lo], right_y),
            5: ((hi, y_l), ryn.at[1, hi], left_y),
        }[i]
        return remote(dense.at[src], dst, ys.at[g], yr.at[g, i if i < 2 else 2], to)

    def y_direct(g, h):
        ps = pl.ds(*GROUPS[g])
        yy = lax.rem(y + h, NY)
        return remote(dense.at[ps, yy], ryd.at[h - 1, ps], ys.at[g], yr.at[g, 2], dev(z, yy, core, red))

    def y_copies(g, which):
        if RELAYED[g]:
            return [y_copy(g, i) for i in which]
        return [y_direct(g, h) for h in (2, 1, 3)]

    def y_second(g):
        lo, hi = y_halves(g)
        y_copy(g, 0).wait_recv()
        dense[lo, y_r] += ryo[lo]
        y_copy(g, 4).start()
        y_copy(g, 1).wait_recv()
        dense[hi, y_l] += ryo[hi]
        y_copy(g, 5).start()

    def densify(g):
        p0, n = GROUPS[g]
        core_copy(g).wait_recv()
        for p in range(p0, p0 + n, 2):
            own = jnp.concatenate([parts4[red, p], parts4[red, p + 1]], axis=1)
            oth = jnp.concatenate([coreacc[p], coreacc[p + 1]], axis=1)
            both = jnp.concatenate([own, oth], axis=0)
            high = both.astype(BF)
            rest = (both - high.astype(F32)).astype(BF)
            d = jnp.dot(place2, jnp.concatenate([high, rest], axis=0), preferred_element_type=F32)
            dense[p] = d[:, :NQ].reshape(NY, KEYS, NQ)
            dense[p + 1] = d[:, NQ:].reshape(NY, KEYS, NQ)
        for c in y_copies(g, range(4)):
            c.start()

    def z_rows(g):
        p0, n = GROUPS[g]
        return pl.ds(p0 * SLOTS, n * SLOTS)

    def z_copy(g, h):
        zz = lax.rem(z + h, NZ)
        at = z_rows(g)
        return remote(zbuf.at[zz, at], zrecv.at[z, at], zs.at[g], zr.at[g], dev(zz, y, core, red))

    def z_all(g):
        every = zrecv.at[pl.ds(0, NZ - 1), z_rows(g)]
        return remote(every, every, zs.at[g], zr.at[g], other)

    zflat = zbuf.reshape(NZ * SLOTS * PQ, NQ)

    def y_last(g):
        p0, n = GROUPS[g]
        late = (ryn if RELAYED[g] else ryd).at[:, pl.ds(p0, n)]
        remote(late, late, ys.at[g], yr.at[g, 2], other).wait_recv()
        for i in range(n):
            p = p0 + i
            total = dense[p, y]
            if RELAYED[g]:
                total = total + (ryn[0, p] + ryn[1, p])
            else:
                total = total + (ryd[0, p] + ryd[1, p] + ryd[2, p])
            for zz in range(NZ):
                zflat[pl.ds(zz * SLOTS * PQ + p0 * SLOTS + i, SLOTS, stride=n), :] = total[zz * SLOTS : (zz + 1) * SLOTS]
        for h in (4, 3, 5, 2, 6, 1, 7):
            z_copy(g, h).start()

    def z_last(g):
        p0, n = GROUPS[g]
        z_all(g).wait_recv()
        at = z_rows(g)
        total = zbuf[z, at]
        for h in range(1, NZ):
            total = total + zrecv[lax.rem(z + h, NZ), at]
        lo, i0 = p0 // 8, p0 % 8
        for slot in range(SLOTS):
            outf[pl.ds(slot * PQ + 2 * i0 + lo, n, stride=2), :] = total[slot * n : (slot + 1) * n]

    def x_sent(g):
        sent = parts4.at[pl.ds(0, 3), pl.ds(*GROUPS[g])]
        remote(sent, sent, xs.at[g], xl.at[g], other).wait_send()
        core_copy(g).wait_send()

    many(0, NCH - 3, NCH)
    x_first(2, 0)
    many(1, 0, CHUNKS[1])
    x_last(0)
    densify(0)
    x_second(2, 0)
    y_second(0)
    x_last(1)
    densify(1)
    x_last(2)
    densify(2)
    y_last(0)
    x_sent(0)
    x_sent(1)
    x_sent(2)
    y_last(1)
    y_last(2)
    z_last(0)
    z_last(1)
    z_last(2)
    out_ref[...] = outf[...].astype(BF).reshape(SLOTS, PQ, NQ)

    for g in range(NG):
        sent = dense.at[pl.ds(*GROUPS[g]), pl.ds(0, 3)]
        remote(sent, sent, ys.at[g], yr.at[g, 2], other).wait_send()
        z_all(g).wait_send()


def shards(
    ints, block_pairs, block_dest, block_slot, occ_density, virt_density, isdf_cols, slab_cols
):
    hbm = pl.BlockSpec(memory_space=pl.ANY)
    vmem = pl.BlockSpec(memory_space=pltpu.VMEM)
    dma = pltpu.SemaphoreType.DMA
    pairs_t = block_pairs.T
    return pl.pallas_call(
        kernel,
        out_shape=jax.ShapeDtypeStruct((SLOTS, PQ, NQ), BF),
        in_specs=[hbm] * 8,
        out_specs=vmem,
        scratch_shapes=[
            pltpu.SMEM((2, NB), jnp.int32),
            pltpu.VMEM((2, NB), jnp.int32),
            pltpu.VMEM((1, NB), jnp.int32),
            pltpu.VMEM((1, NB), jnp.int32),
            pltpu.VMEM((1, NQ), jnp.int32),
            pltpu.VMEM((NB, LAM, BA * BA), BF),
            pltpu.VMEM((BA * BA, NAB), BF),
            pltpu.VMEM((LAM * BA, NAB), BF),
            pltpu.VMEM((NAB, BA, NCAND), BF),
            pltpu.VMEM((NB, BA * BA), F32),
            pltpu.VMEM((NB, LAM * BA), F32),
            pltpu.VMEM((CB * BA, 2 * BA), F32),
            pltpu.VMEM((CB * LAM, 2 * BA), F32),
            pltpu.VMEM((NB, 2 * BA, 2 * NQ), BF),
            pltpu.VMEM((NB, LAM, NQ), F32),
            pltpu.VMEM((NX * PQ * NB, NQ), F32),
            pltpu.VMEM((PQ, NB, NQ), F32),
            pltpu.VMEM((2, PQ, NB, NQ), F32),
            pltpu.VMEM((8, 128), jnp.int32),
            pltpu.VMEM((8, 128), jnp.int32),
            pltpu.VMEM((PQ, NB, NQ), F32),
            pltpu.VMEM((PQ, NY, KEYS, NQ), F32),
            pltpu.VMEM((PQ, KEYS, NQ), F32),
            pltpu.VMEM((2, PQ, KEYS, NQ), F32),
            pltpu.VMEM((NY - 1, PQ, KEYS, NQ), F32),
            pltpu.VMEM((NZ, SLOTS * PQ, NQ), F32),
            pltpu.VMEM((NZ, SLOTS * PQ, NQ), F32),
            pltpu.VMEM((SLOTS * PQ, NQ), F32),
            dma((5,)),
            dma((4,)),
            dma((NCH,)),
            dma((NG,)),
            dma((2 * sum(CHUNKS),)),
            dma((NG,)),
            dma((NG,)),
            dma((NG,)),
            dma((1,)),
            dma((1,)),
            dma((NG,)),
            dma((NG, 3)),
            dma((NG,)),
            dma((NG,)),
        ],
        compiler_params=pltpu.CompilerParams(
            collective_id=0, has_side_effects=True, vmem_limit_bytes=56 * 1024 * 1024
        ),
        cost_estimate=pl.CostEstimate(flops=3_000_000_000, bytes_accessed=14_000_000, transcendentals=0),
    )(
        ints,
        pairs_t,
        block_dest.reshape(1, NB),
        block_slot.reshape(1, NB),
        slab_cols.reshape(1, NQ),
        occ_density.transpose(1, 2, 0).reshape(BA * BA, NAB),
        virt_density.transpose(1, 2, 0).reshape(BA * BA, NAB),
        isdf_cols,
    )


def solution(mesh):
    return jax.shard_map(
        shards,
        mesh=mesh,
        in_specs=(
            P("pair", "red", None),
            P("pair", None),
            P("pair", None),
            P("pair"),
            P(),
            P(),
            P(),
            P(),
        ),
        out_specs=P("pair", "red", None),
        check_vma=False,
    )
```
